256 devices in a mesh: phase: 4 (over y), rep: 8 (over z), tp: 8 (over x, core).
Axes of the slice: x: 4, y: 4, z: 8, core: 2. Of those that a mesh axis runs over, the one named last changes fastest.
Arguments:
- patches: bfloat16 [32768, 1280], P(('phase', 'rep')), may hold values from -160 to 160
- window_order: int32 [32, 1024], P(('phase', 'rep')), may hold values from 0 to 1023, each once within a row
- vis_gain: float32 [1280], replicated, may hold values from 0.5 to 1.5
- vis_qkv: bfloat16 [1280, 3840], P(None, 'tp'), may hold values from -0.15625 to 0.15625
- vis_qkv_bias: float32 [3840], P('tp'), may hold values from -6 to 6
- vis_proj: bfloat16 [1280, 1280], P('tp'), may hold values from -0.625 to 0.625
- vis_proj_bias: float32 [1280], replicated, may hold values from -3 to 3
- merge_gain: float32 [1280], replicated, may hold values from 0.5 to 1.5
- img_owner: int32 [32, 16], P(('phase', 'rep')), may hold values from 0 to 31, as said below
- img_slot: int32 [32, 16], P(('phase', 'rep')), may hold values from 0 to 31, as said below
- prompt_rows: bfloat16 [16384, 8192], P(('phase', 'rep'), 'tp'), may hold values from -160 to 160
- lang_gain: float32 [8192], replicated, may hold values from 0.5 to 1.5
- w_query: bfloat16 [8192, 4096], P(('phase', 'rep'), 'tp'), may hold values from -0.0625 to 0.0625
- b_query: float32 [4096], P('tp'), may hold values from -6 to 6
- w_key: bfloat16 [8192, 1024], P(('phase', 'rep'), 'tp'), may hold values from -0.0625 to 0.0625
- b_key: float32 [1024], P('tp'), may hold values from -6 to 6
- w_value: bfloat16 [8192, 1024], P(('phase', 'rep'), 'tp'), may hold values from -0.0625 to 0.0625
- b_value: float32 [1024], P('tp'), may hold values from -2.5 to 2.5
- page_owner: int32 [32, 16], P(('phase', 'rep')), may hold values from 0 to 7, as said below
- page_slot: int32 [32, 16], P(('phase', 'rep')), may hold values from 0 to 15, as said below
Outputs:
- image_buffer: bfloat16 [16384, 5120], P(('phase', 'rep'), 'tp')
- attn_out: bfloat16 [16384, 4096], P(('phase', 'rep'), 'tp')
- kv_pool: bfloat16 [512, 32, 2048], P(('phase', 'rep'), None, 'tp')
The draws below stay inside these ranges and needn't reach their ends.
Inputs may be any that keep to these rules, and one draw needn't show every extreme that they name: `window_order`: each row lists every index of its block once. `img_owner`: the 16 requests of one block go to distinct owners; an owner receives at most 32 requests in all, and some owner exactly 32. `img_slot`: requests sent to one owner take distinct slots. `page_owner`: each block holds 4 prompts of whole pages, each prompt's pages going to one owner and the prompts of a block to distinct owners; within one phase every block has the same prompt lengths in the same order, 5, 5, 3 and 3 pages in an order drawn for the phase, so at most 5 pages go from one block to one owner, and every owner receives exactly 16 pages. `page_slot`: the pages that reach one owner take distinct slots.
All inputs are finite; a program needn't handle non-finite values.
Results may differ from the reference program's by a relative error of at most 0.013.
Values may be sent and summed in bfloat16 or wider, within the bound.
No kernel may reach another device: no remote copies, remote signals or barrier semaphores. Data moves between devices by JAX's collectives and lax.ppermute only.
A program may use at most 128 MiB of HBM per device.

```python
import jax
import jax.numpy as jnp
from jax import lax

VD = 1280
VH = 16
WIN = 64
REQ_IMG = 16
D = 8192
QH = 32
KVH = 8
HD = 128
PAGE = 32
PAGES_DEV = 16
PATCH_DEV = 1024
GROUPS = 32
SLOTB = 32
ROWS = 512
ALL_PATCH = 32768
ALL_ROWS = 16384
N_PHASE = 4
N_REP = 8


def spread_values(subkey, row_total, col_total):
    key_rows, key_cols, key_normal = jax.random.split(subkey, 3)
    row_scale = jnp.exp(jax.random.uniform(key_rows, (row_total, 1), jnp.float32) * jnp.log(10.0))
    col_scale = jnp.exp(jax.random.uniform(key_cols, (1, col_total), jnp.float32, -1.2, 1.1))
    normal_vals = jnp.clip(jax.random.normal(key_normal, (row_total, col_total), jnp.float32), -4.0, 4.0)
    base = normal_vals
    return (base * row_scale * col_scale).astype(jnp.bfloat16)


def image_routes(subkey):
    key_order, key_slots = jax.random.split(subkey)
    owner_order = jax.random.permutation(key_order, GROUPS)
    source = jnp.arange(GROUPS, dtype=jnp.int32)[:, None]
    request = jnp.arange(REQ_IMG, dtype=jnp.int32)[None, :]
    hot_idx = (source + request) % 8
    cold_idx = 8 + (source + request) % (GROUPS - 8)
    target_idx = jnp.where(request < 8, hot_idx, cold_idx)
    flat_idx = target_idx.T.reshape(-1)
    item_iota = jnp.arange(flat_idx.shape[0], dtype=jnp.int32)
    earlier = item_iota[:, None] > item_iota[None, :]
    rank_in = jnp.sum(((flat_idx[:, None] == flat_idx[None, :]) & earlier).astype(jnp.int32), axis=1)
    rank_in = rank_in.reshape(REQ_IMG, GROUPS).T
    slot_perms = jax.vmap(lambda sub: jax.random.permutation(sub, SLOTB))(jax.random.split(key_slots, GROUPS))
    slot_ids = slot_perms[target_idx, rank_in]
    return (owner_order[target_idx].astype(jnp.int32), slot_ids.astype(jnp.int32))


def page_routes(subkey):
    key_lengths, key_owner, key_slots = jax.random.split(subkey, 3)
    pattern = jnp.array([5, 5, 3, 3], dtype=jnp.int32) * (PAGES_DEV // 16)
    lengths = jax.vmap(lambda sub: jax.random.permutation(sub, pattern))(jax.random.split(key_lengths, N_PHASE))
    prompt_ends = jnp.cumsum(lengths, axis=1)
    page_iota = jnp.arange(PAGES_DEV, dtype=jnp.int32)
    prompt_ids = jnp.sum((page_iota[None, :, None] >= prompt_ends[:, None, :]).astype(jnp.int32), axis=2)
    owner_order = jax.vmap(lambda sub: jax.random.permutation(sub, N_REP))(jax.random.split(key_owner, N_PHASE))
    source = jnp.arange(N_REP, dtype=jnp.int32)
    local_idx = (source[None, :, None] + prompt_ids[:, None, :]) % N_REP
    phase_iota = jnp.arange(N_PHASE, dtype=jnp.int32)[:, None, None]
    owner_ids = owner_order[phase_iota, local_idx]
    slot_perms = jax.vmap(lambda sub: jax.random.permutation(sub, PAGES_DEV))(jax.random.split(key_slots, N_PHASE * N_REP))
    slot_perms = slot_perms.reshape(N_PHASE, N_REP, PAGES_DEV)
    slot_ids = slot_perms[phase_iota, owner_ids, page_iota[None, None, :]]
    return (owner_ids.reshape(GROUPS, PAGES_DEV).astype(jnp.int32), slot_ids.reshape(GROUPS, PAGES_DEV).astype(jnp.int32))


def draw_patches(key, part):
    key = jax.random.fold_in(key, 1)
    return spread_values(key, ALL_PATCH, VD)


def draw_prompt_rows(key, part):
    key = jax.random.fold_in(key, 2)
    return spread_values(key, ALL_ROWS, D)


def draw_img_owner(key, part):
    owner_ids, slot_ids = image_routes(key)
    return owner_ids


def draw_img_slot(key, part):
    owner_ids, slot_ids = image_routes(key)
    return slot_ids


def draw_page_owner(key, part):
    owner_ids, slot_ids = page_routes(key)
    return owner_ids


def draw_page_slot(key, part):
    owner_ids, slot_ids = page_routes(key)
    return slot_ids


def draw_b_query(key, part):
    key = jax.random.fold_in(key, 7)
    noise = jnp.clip(jax.random.normal(key, (QH * HD,), jnp.float32), -3.0, 3.0)
    return 0.5 * noise


def draw_b_key(key, part):
    key = jax.random.fold_in(key, 8)
    noise = jnp.clip(jax.random.normal(key, (KVH * HD,), jnp.float32), -3.0, 3.0)
    return 0.5 * noise


def draw_vis_qkv_bias(key, part):
    key = jax.random.fold_in(key, 9)
    key_noise = jax.random.fold_in(key, 0)
    noise = jnp.clip(jax.random.normal(key_noise, (VH, 3, VD // VH), jnp.float32), -3.0, 3.0)
    return (0.5 * noise).reshape(-1)


def block_scale(own_key, extent, cuts, low, top_value):
    factor_of, own = 1.0, jax.random.fold_in(own_key, 6)
    for axis_at, blocks in cuts:
        draws = jnp.exp(jax.random.uniform(jax.random.fold_in(own, axis_at), (blocks,), jnp.float32, low / len(cuts), top_value / len(cuts)))
        factor_of = factor_of * jnp.repeat(draws, extent[axis_at] // blocks).reshape([-1 if axis == axis_at else 1 for axis in range(len(extent))])
    return factor_of


def bell_draw(key, shape, spread, most, pieces=(), kind=jnp.bfloat16):
    factor_of = block_scale(key, shape, pieces, -0.22, 0.18) if pieces else 1.0
    entries = jax.random.normal(key, shape, jnp.float32) * spread * factor_of
    return jnp.minimum(jnp.maximum(entries, -most), most).astype(kind)


def setup_inputs(seed: int = 0) -> dict:
    arg_keys = jax.random.split(jax.random.key(seed), 21)
    return {
        "patches": draw_patches(jax.random.fold_in(arg_keys[20], 71), 0),
        "window_order": jax.vmap(lambda own: jax.random.permutation(own, PATCH_DEV))(jax.random.split(arg_keys[1], GROUPS)).reshape((GROUPS, PATCH_DEV)).astype(jnp.int32),
        "vis_gain": jnp.clip(1.0 + 0.1 * jax.random.normal(arg_keys[2], (VD,), jnp.float32), 0.5, 1.5),
        "vis_qkv": bell_draw(arg_keys[3], (VD, 3 * VD), VD ** -0.5, 0.15625, ((1, 8),)),
        "vis_qkv_bias": draw_vis_qkv_bias(jax.random.fold_in(arg_keys[20], 71), 0),
        "vis_proj": bell_draw(arg_keys[5], (VD, VD), (VD // 16) ** -0.5, 0.625, ((0, 8),)),
        "vis_proj_bias": bell_draw(arg_keys[6], (VD,), 0.3, 3.0, (), jnp.float32),
        "merge_gain": jnp.clip(1.0 + 0.1 * jax.random.normal(arg_keys[7], (VD,), jnp.float32), 0.5, 1.5),
        "img_owner": draw_img_owner(jax.random.fold_in(arg_keys[20], 71), 0),
        "img_slot": draw_img_slot(jax.random.fold_in(arg_keys[20], 71), 0),
        "prompt_rows": draw_prompt_rows(jax.random.fold_in(arg_keys[20], 71), 0),
        "lang_gain": jnp.clip(1.0 + 0.1 * jax.random.normal(arg_keys[11], (D,), jnp.float32), 0.5, 1.5),
        "w_query": bell_draw(arg_keys[12], (D, QH * HD), D ** -0.5, 0.0625, ((0, 32), (1, 8))),
        "b_query": draw_b_query(jax.random.fold_in(arg_keys[20], 71), 0),
        "w_key": bell_draw(arg_keys[14], (D, KVH * HD), D ** -0.5, 0.0625, ((0, 32), (1, 8))),
        "b_key": draw_b_key(jax.random.fold_in(arg_keys[20], 71), 0),
        "w_value": bell_draw(arg_keys[16], (D, KVH * HD), D ** -0.5, 0.0625, ((0, 32), (1, 8))),
        "b_value": bell_draw(arg_keys[17], (KVH * HD,), 0.5, 2.5, ((0, 8),), jnp.float32),
        "page_owner": draw_page_owner(jax.random.fold_in(arg_keys[20], 71), 0),
        "page_slot": draw_page_slot(jax.random.fold_in(arg_keys[20], 71), 0),
    }


def rms_norm(inputs, scale_gain):
    inputs = inputs.astype(jnp.float32)
    factor = lax.rsqrt(lax.optimization_barrier(jnp.mean(inputs * inputs, axis=-1, keepdims=True)) + 1e-06)
    return inputs * factor * scale_gain

def softmax_rows(scores):
    row_max = lax.optimization_barrier(jnp.max(scores, axis=-1, keepdims=True))
    raised = jnp.exp(scores - row_max)
    return raised / lax.optimization_barrier(jnp.sum(raised, axis=-1, keepdims=True))

def rounded(inputs):
    return lax.optimization_barrier(inputs.astype(jnp.bfloat16)).astype(jnp.float32)

def rotate(inputs, position):
    half_dim = inputs.shape[-1] // 2
    inv_freq = jnp.exp(-jnp.log(1000000.0) * jnp.arange(half_dim).astype(jnp.float32) / half_dim)
    angles = position.astype(jnp.float32)[:, None] * inv_freq[None, :]
    cosine = jnp.cos(angles)[:, None, :]
    sines = jnp.sin(angles)[:, None, :]
    lower_half = inputs[..., :half_dim]
    upper_half = inputs[..., half_dim:]
    return jnp.concatenate([lower_half * cosine - upper_half * sines, upper_half * cosine + lower_half * sines], axis=-1)

def prompt_layout(owner_ids, page_rows):
    page_total = owner_ids.shape[0]
    page_iota = jnp.arange(page_total, dtype=jnp.int32)
    page_starts = jnp.concatenate([jnp.ones((1,), dtype=bool), owner_ids[1:] != owner_ids[:-1]])
    prompt_ids = jnp.cumsum(page_starts.astype(jnp.int32))
    first_page = lax.cummax(jnp.where(page_starts, page_iota, 0), axis=0)
    segment = jnp.repeat(prompt_ids, page_rows)
    position = jnp.arange(page_total * page_rows, dtype=jnp.int32) - jnp.repeat(first_page, page_rows) * page_rows
    return (segment, position)

def attend(query_rows, key_rows, value_rows, segment):
    row_total, head_total, head_dim = query_rows.shape
    kv_heads = key_rows.shape[1]
    grouped = query_rows.astype(jnp.float32).reshape(row_total, kv_heads, head_total // kv_heads, head_dim)
    scores = jnp.einsum('qgjd,kgd->gjqk', grouped, key_rows.astype(jnp.float32)) * head_dim ** (-0.5)
    iota_rows = jnp.arange(row_total)
    allowed = (segment[:, None] == segment[None, :]) & (iota_rows[None, :] <= iota_rows[:, None])
    scores = jnp.where(allowed, scores, -1e+30)
    weights = rounded(softmax_rows(scores))
    mixed = jnp.einsum('gjqk,kgd->qgjd', weights, value_rows.astype(jnp.float32))
    return mixed.reshape(row_total, head_total * head_dim).astype(jnp.bfloat16)

def vision_block(patch_rows, order_ids, vis_gain, vis_qkv, vis_qkv_bias, vis_proj, vis_proj_bias, merge_gain):
    window_rows = jnp.take(patch_rows, order_ids, axis=0)
    normed = rms_norm(window_rows, vis_gain).astype(jnp.bfloat16)
    projected = rounded(jnp.dot(normed, vis_qkv, preferred_element_type=jnp.float32) + vis_qkv_bias)
    head_dim = VD // VH
    qkv_parts = projected.reshape(REQ_IMG, WIN, VH, 3, head_dim)
    scores = jnp.einsum('wqhd,wkhd->whqk', qkv_parts[..., 0, :], qkv_parts[..., 1, :]) * head_dim ** (-0.5)
    weights = rounded(softmax_rows(scores))
    vis_heads = jnp.einsum('whqk,wkhd->wqhd', weights, qkv_parts[..., 2, :]).astype(jnp.bfloat16)
    vis_heads = vis_heads.reshape(PATCH_DEV, VD)
    mixed = window_rows.astype(jnp.float32) + jnp.dot(vis_heads, vis_proj, preferred_element_type=jnp.float32) + vis_proj_bias
    merged = rms_norm(mixed, merge_gain).astype(jnp.bfloat16)
    return merged.reshape(REQ_IMG, WIN // 4, 4 * VD)

def language_block(prompt_block, owner_ids, lang_gain, w_query, b_query, w_key, b_key, w_value, b_value):
    normed = rms_norm(prompt_block, lang_gain).astype(jnp.bfloat16)
    query = jnp.dot(normed, w_query, preferred_element_type=jnp.float32) + b_query
    keyed = jnp.dot(normed, w_key, preferred_element_type=jnp.float32) + b_key
    valued = jnp.dot(normed, w_value, preferred_element_type=jnp.float32) + b_value
    row_total = prompt_block.shape[0]
    page_rows = row_total // owner_ids.shape[0]
    segment, position = prompt_layout(owner_ids, page_rows)
    query_rot = lax.optimization_barrier(rotate(query.reshape(row_total, QH, HD), position).astype(jnp.bfloat16))
    key_rot = lax.optimization_barrier(rotate(keyed.reshape(row_total, KVH, HD), position).astype(jnp.bfloat16))
    value_rows = lax.optimization_barrier(valued.reshape(row_total, KVH, HD).astype(jnp.bfloat16))
    heads_out = attend(query_rot, key_rot, value_rows, segment)
    kv_pages = jnp.stack([key_rot, value_rows], axis=2).reshape(owner_ids.shape[0], page_rows, 2 * KVH * HD)
    return (heads_out, kv_pages)

def reference(patches, window_order, vis_gain, vis_qkv, vis_qkv_bias, vis_proj, vis_proj_bias, merge_gain, img_owner, img_slot, prompt_rows, lang_gain, w_query, b_query, w_key, b_key, w_value, b_value, page_owner, page_slot):
    patch_blocks = patches.reshape(GROUPS, PATCH_DEV, VD)

    def encode(inputs):
        return vision_block(inputs[0], inputs[1], vis_gain, vis_qkv, vis_qkv_bias, vis_proj, vis_proj_bias, merge_gain)
    merged = lax.map(encode, (patch_blocks, window_order))
    merged = merged.reshape(GROUPS * REQ_IMG, WIN // 4, 4 * VD)
    buffer = jnp.zeros((GROUPS, SLOTB, WIN // 4, 4 * VD), jnp.bfloat16)
    buffer = buffer.at[img_owner.reshape(-1), img_slot.reshape(-1)].set(merged)
    image_buffer = buffer.reshape(GROUPS * SLOTB * (WIN // 4), 4 * VD)
    prompt_blocks = prompt_rows.reshape(GROUPS, ROWS, D)

    def prefill(inputs):
        return language_block(inputs[0], inputs[1], lang_gain, w_query, b_query, w_key, b_key, w_value, b_value)
    heads_out, kv_pages = lax.map(prefill, (prompt_blocks, page_owner))
    attn_out = heads_out.reshape(GROUPS * ROWS, QH * HD)
    phase_of = jnp.arange(GROUPS, dtype=jnp.int32) // N_REP
    target = (phase_of[:, None] * N_REP + page_owner) * PAGES_DEV + page_slot
    kv_pool = jnp.zeros((GROUPS * PAGES_DEV, PAGE, 2 * KVH * HD), jnp.bfloat16)
    kv_pool = kv_pool.at[target.reshape(-1)].set(kv_pages.reshape(GROUPS * PAGES_DEV, PAGE, 2 * KVH * HD))
    return (image_buffer, attn_out, kv_pool)
```

```python
import jax
import jax.numpy as jnp
import numpy as np
from jax import lax
from jax.experimental import pallas as pl
from jax.experimental.pallas import tpu as pltpu
from jax.sharding import PartitionSpec as P

VD = 1280
VHD = 80
LANE = 128
HD = 128
EPS = 1e-06
CAP = 5
WINDOW = 384
VMEM_LIMIT = 40 * 1024 * 1024


def whole(shape):
    return pl.BlockSpec(shape, lambda *_: (0,) * len(shape))


def params(limit=VMEM_LIMIT):
    return pltpu.CompilerParams(vmem_limit_bytes=limit)


def shift(axis, by):
    n = lax.axis_size(axis)
    return lambda a: lax.ppermute(a, axis, [(i, (i + by) % n) for i in range(n)])


def vision_kernel(core_ref, rows_ref, gain_ref, w_ref, bias_ref, proj_ref, keep_ref, send_ref):
    parts, span, width = rows_ref.shape
    total = parts * span
    rows = rows_ref[...].reshape(total, width).astype(jnp.float32)
    factor = lax.rsqrt(jnp.mean(rows * rows, axis=-1, keepdims=True) + EPS)
    normed = (rows * factor * gain_ref[...]).astype(jnp.bfloat16)
    projected = jnp.dot(normed, w_ref[...], preferred_element_type=jnp.float32) + bias_ref[...]
    projected = projected.astype(jnp.bfloat16)
    window_q = lax.broadcasted_iota(jnp.int32, (total, total), 0) % span // 16
    window_k = lax.broadcasted_iota(jnp.int32, (total, total), 1) % span // 16
    same = window_q == window_k
    heads = []
    for head in range(projected.shape[1] // (3 * LANE)):
        at = head * 3 * LANE
        query = projected[:, at : at + LANE]
        keyed = projected[:, at + LANE : at + 2 * LANE]
        valued = projected[:, at + 2 * LANE : at + 3 * LANE]
        scores = lax.dot_general(
            query, keyed, (((1,), (1,)), ((), ())), preferred_element_type=jnp.float32
        ) * (VHD ** (-0.5))
        scores = jnp.where(same, scores, -1e30)
        raised = jnp.exp(scores - jnp.max(scores, axis=-1, keepdims=True))
        weights = (raised / jnp.sum(raised, axis=-1, keepdims=True)).astype(jnp.bfloat16)
        heads.append(
            jnp.dot(weights, valued, preferred_element_type=jnp.float32).astype(jnp.bfloat16)
        )
    mixed = jnp.concatenate(heads, axis=1)
    half = width // 2
    core = core_ref[0]
    mine = pl.multiple_of(core * half, LANE)
    other = pl.multiple_of((1 - core) * half, LANE)
    for out_ref, at in ((keep_ref, mine), (send_ref, other)):
        part = jnp.dot(mixed, proj_ref[:, pl.ds(at, half)], preferred_element_type=jnp.float32)
        out_ref[...] = part.astype(jnp.bfloat16).reshape(parts, span, half)


def vision_partial(rows, gain, w_pad, bias_pad, proj_pad, core):
    parts, span, width = rows.shape
    step = 64
    half = width // 2
    spec = pl.BlockSpec((parts, step, half), lambda i, _: (0, i, 0))
    out = jax.ShapeDtypeStruct((parts, span, half), jnp.bfloat16)
    return pl.pallas_call(
        vision_kernel,
        grid_spec=pltpu.PrefetchScalarGridSpec(
            num_scalar_prefetch=1,
            grid=(span // step,),
            in_specs=[
                pl.BlockSpec((parts, step, width), lambda i, _: (0, i, 0)),
                whole(gain.shape),
                whole(w_pad.shape),
                whole(bias_pad.shape),
                whole(proj_pad.shape),
            ],
            out_specs=[spec, spec],
        ),
        out_shape=[out, out],
        compiler_params=params(),
        cost_estimate=pl.CostEstimate(
            flops=2 * parts * span * width * 1024, bytes_accessed=8_000_000, transcendentals=0
        ),
    )(core, rows, gain, w_pad, bias_pad, proj_pad)


def place_kernel(at_ref, items_ref, out_ref):
    out_ref[...] = jnp.zeros_like(out_ref)
    for item in range(items_ref.shape[0]):
        at = at_ref[item]

        @pl.when(at >= 0)
        def _():
            out_ref[pl.ds(at, 1)] = items_ref[item : item + 1]


def place(at, items, slots):
    shape = (slots,) + items.shape[1:]
    return pl.pallas_call(
        place_kernel,
        grid_spec=pltpu.PrefetchScalarGridSpec(
            num_scalar_prefetch=1,
            grid=(1,),
            in_specs=[whole(items.shape)],
            out_specs=whole(shape),
        ),
        out_shape=jax.ShapeDtypeStruct(shape, items.dtype),
        compiler_params=params(),
    )(at, items)


def columns(x_ref, offsets_ref, units):
    return jnp.concatenate(
        [
            x_ref[:, pl.ds(pl.multiple_of(offsets_ref[unit] * LANE, LANE), LANE * count)]
            for unit, count in units
        ],
        axis=1,
    )


def rotary(values, cosine, sines):
    return values * cosine + pltpu.roll(values, HD // 2, 1) * sines


def kv_kernel(units, offsets_ref, x_ref, factor_ref, bias_ref, cos_ref, sin_ref, *refs):
    pieces, out_ref = refs[:-1], refs[-1]
    total = jnp.zeros((x_ref.shape[0], pieces[0].shape[1]), jnp.float32)
    for piece_ref, own in zip(pieces, units):
        total += jnp.dot(
            columns(x_ref, offsets_ref, own), piece_ref[...], preferred_element_type=jnp.float32
        )
    total = total * factor_ref[...] + bias_ref[...]
    out_ref[:, :HD] = rotary(total[:, :HD], cos_ref[...], sin_ref[...]).astype(jnp.bfloat16)
    out_ref[:, HD:] = total[:, HD:].astype(jnp.bfloat16)


def kv_rows(offsets, x, factor, bias, cosine, sines, pieces, units):
    rows, depth = x.shape
    step = 128
    by_rows = lambda width: pl.BlockSpec((step, width), lambda i, _: (i, 0))
    width = pieces[0].shape[1]
    return pl.pallas_call(
        lambda *refs: kv_kernel(units, *refs),
        grid_spec=pltpu.PrefetchScalarGridSpec(
            num_scalar_prefetch=1,
            grid=(rows // step,),
            in_specs=[by_rows(depth), by_rows(1), whole(bias.shape), by_rows(HD), by_rows(HD)]
            + [whole(piece.shape) for piece in pieces],
            out_specs=by_rows(width),
        ),
        out_shape=jax.ShapeDtypeStruct((rows, width), jnp.bfloat16),
        compiler_params=params(),
        cost_estimate=pl.CostEstimate(
            flops=2 * rows * depth * width, bytes_accessed=13_000_000, transcendentals=0
        ),
    )(offsets, x, factor, bias, cosine, sines, *pieces)


def query_kernel(units, tail_units, offsets_ref, x_ref, *refs):
    pieces, out_ref, tail_ref = refs[:-2], refs[-2], refs[-1]
    total = jnp.zeros(out_ref.shape, jnp.float32)
    for piece_ref, own in zip(pieces, units):
        total += jnp.dot(
            columns(x_ref, offsets_ref, own), piece_ref[...], preferred_element_type=jnp.float32
        )
    out_ref[...] = total
    tail_ref[...] = columns(x_ref, offsets_ref, tail_units)


def query_sums(offsets, x, pieces, units, tail_units, tail_width):
    rows, depth = x.shape
    step = 128
    by_rows = lambda width: pl.BlockSpec((step, width), lambda i, _: (i, 0))
    width = pieces[0].shape[1]
    return pl.pallas_call(
        lambda *refs: query_kernel(units, tail_units, *refs),
        grid_spec=pltpu.PrefetchScalarGridSpec(
            num_scalar_prefetch=1,
            grid=(rows // step,),
            in_specs=[by_rows(depth)] + [whole(piece.shape) for piece in pieces],
            out_specs=[by_rows(width), by_rows(tail_width)],
        ),
        out_shape=[
            jax.ShapeDtypeStruct((rows, width), jnp.float32),
            jax.ShapeDtypeStruct((rows, tail_width), jnp.bfloat16),
        ],
        compiler_params=params(),
        cost_estimate=pl.CostEstimate(
            flops=2 * rows * depth * width, bytes_accessed=18_000_000, transcendentals=0
        ),
    )(offsets, x, *pieces)


def attend_kernel(
    sums_ref, tail_ref, first_ref, second_ref, factor_ref, bias_ref, cos_ref, sin_ref, start_ref,
    kv_ref, out_ref,
):
    step = sums_ref.shape[0]
    split = first_ref.shape[0]
    block = pl.program_id(0)
    total = (
        sums_ref[...]
        + jnp.dot(tail_ref[:, :split], first_ref[...], preferred_element_type=jnp.float32)
        + jnp.dot(tail_ref[:, split:], second_ref[...], preferred_element_type=jnp.float32)
    )
    total = total * factor_ref[...] + bias_ref[...]
    heads = total.shape[1] // HD
    query = jnp.concatenate(
        [
            rotary(total[:, h * HD : (h + 1) * HD], cos_ref[...], sin_ref[...]).astype(jnp.bfloat16)
            for h in range(heads)
        ],
        axis=0,
    )
    begin = pl.multiple_of(jnp.maximum(block * step + step - WINDOW, 0), LANE)
    keyed = kv_ref[pl.ds(begin, WINDOW), :HD]
    valued = kv_ref[pl.ds(begin, WINDOW), HD:]
    scores = lax.dot_general(
        query, keyed, (((1,), (1,)), ((), ())), preferred_element_type=jnp.float32
    ) * (HD ** (-0.5))
    key_at = begin + lax.broadcasted_iota(jnp.int32, (step, WINDOW), 1)
    row_at = block * step + lax.broadcasted_iota(jnp.int32, (step, WINDOW), 0)
    allowed = (key_at <= row_at) & (key_at >= start_ref[...])
    for h in range(heads):
        own = jnp.where(allowed, scores[h * step : (h + 1) * step], -1e30)
        raised = jnp.exp(own - jnp.max(own, axis=-1, keepdims=True))
        weights = (raised / jnp.sum(raised, axis=-1, keepdims=True)).astype(jnp.bfloat16)
        mixed = jnp.dot(weights, valued, preferred_element_type=jnp.float32)
        out_ref[:, h * HD : (h + 1) * HD] = mixed.astype(jnp.bfloat16)


def attend(sums, tail, first, second, factor, bias, cosine, sines, start, kv):
    rows, width = sums.shape
    step = 128
    by_rows = lambda cols: pl.BlockSpec((step, cols), lambda i: (i, 0))
    return pl.pallas_call(
        attend_kernel,
        grid=(rows // step,),
        in_specs=[
            by_rows(width),
            by_rows(tail.shape[1]),
            whole(first.shape),
            whole(second.shape),
            by_rows(1),
            whole(bias.shape),
            by_rows(HD),
            by_rows(HD),
            by_rows(1),
            whole(kv.shape),
        ],
        out_specs=by_rows(width),
        out_shape=jax.ShapeDtypeStruct((rows, width), jnp.bfloat16),
        compiler_params=params(),
    )(sums, tail, first, second, factor, bias, cosine, sines, start, kv)


def gather_query(own):
    up, down = shift("rep", 1), shift("rep", -1)
    fore, back = shift("phase", 1), shift("phase", -1)
    half = own.shape[0] // 2
    up1, down1 = up(own), down(own)
    near = jnp.concatenate([own, up1, down1], axis=0)
    up2, down2 = up(up1), down(down1)
    up3, down3 = up(up2), down(down2)
    up4, down4 = up(up3[:half]), down(down3[half:])
    far = jnp.concatenate([up2, down2, up3, down3, up4, down4], axis=0)
    batches = []
    for batch in (near, far):
        cut = batch.shape[0] // 2
        behind, ahead = fore(batch), back(batch)
        batches.append((batch, behind, ahead, fore(behind[:cut]), back(ahead[cut:])))
    return batches


def gather_kv(own):
    up, down = shift("rep", 1), shift("rep", -1)
    batch = jnp.concatenate(
        [own, shift("phase", 1)(own), shift("phase", -1)(own), shift("phase", 2)(own)], axis=0
    )
    cut = batch.shape[0] // 2
    pieces = [batch]
    rise, fall = batch, batch
    for hop in range(3):
        rise, fall = up(rise), down(fall)
        pieces += [rise, fall]
    return pieces + [up(rise[:cut]), down(fall[cut:])]


def body(
    patches, window_order, vis_gain, vis_qkv, vis_qkv_bias, vis_proj, vis_proj_bias, merge_gain,
    img_owner, img_slot, prompt_rows, lang_gain, w_query, b_query, w_key, b_key, w_value, b_value,
    page_owner, page_slot,
):
    phase, rep, tp = lax.axis_index("phase"), lax.axis_index("rep"), lax.axis_index("tp")
    n_phase, n_rep = lax.axis_size("phase"), lax.axis_size("rep")
    groups = n_phase * n_rep
    group = phase * n_rep + rep
    chip, core = tp // 2, tp % 2
    bf16, f32 = jnp.bfloat16, jnp.float32

    depth = w_query.shape[0]
    gain = lax.dynamic_slice_in_dim(lang_gain, group * depth, depth)[:, None]
    scaled = lambda w: (w.astype(f32) * gain).astype(bf16)
    near, far = gather_query(scaled(w_query))
    kv_pieces = gather_kv(jnp.concatenate([scaled(w_key), scaled(w_value)], axis=1))
    x = lax.all_gather(prompt_rows, "tp", axis=1, tiled=True)

    owner, slot = img_owner[0], img_slot[0]
    owners, slots = page_owner[0], page_slot[0]
    pages = owners.shape[0]
    page_iota = jnp.arange(pages, dtype=jnp.int32)
    same = owners[:, None] == owners[None, :]
    first_page = jnp.min(jnp.where(same, page_iota[None, :], pages), axis=1)
    page_pos = page_iota - first_page
    dest = jnp.arange(groups, dtype=jnp.int32)
    image_label = jnp.sum(
        jnp.where(owner[None, :] == dest[:, None], slot[None, :] + 1, 0), axis=1
    )
    cap_iota = jnp.arange(7, dtype=jnp.int32)
    page_label = jnp.sum(
        jnp.where(
            (phase * n_rep + owners[None, None, :] == dest[:, None, None])
            & (page_pos[None, None, :] == cap_iota[None, :, None]),
            slots[None, None, :] + 1,
            0,
        ),
        axis=2,
    )
    labels = jnp.concatenate([image_label[:, None], page_label], axis=1)
    labels = lax.all_to_all(labels, ("phase", "rep"), split_axis=0, concat_axis=0, tiled=True)
    image_at = labels[:, 0] - 1
    page_at = (lax.dynamic_slice_in_dim(labels, phase * n_rep, n_rep, 0)[:, 1 : 1 + CAP] - 1).reshape(-1)

    patch_count, width = patches.shape
    merge = 4
    order = window_order[0].reshape(patch_count // merge, merge).T.reshape(-1)
    window_rows = jnp.take(patches, order, axis=0).reshape(merge, patch_count // merge, width)
    chunks = vis_qkv.shape[1] // VHD
    spread = np.zeros((chunks * VHD, chunks * LANE), np.float32)
    for at in range(chunks * VHD):
        spread[at, at // VHD * LANE + at % VHD] = 1
    spread = jnp.asarray(spread, bf16)
    w_pad = jnp.dot(vis_qkv, spread, preferred_element_type=f32).astype(bf16)
    bias_pad = jnp.pad(vis_qkv_bias.reshape(chunks, VHD), ((0, 0), (0, LANE - VHD))).reshape(1, -1)
    proj_pad = jnp.pad(
        vis_proj.reshape(-1, VHD, width), ((0, 0), (0, LANE - VHD), (0, 0))
    ).reshape(-1, width)
    keep, send = vision_partial(
        window_rows, vis_gain[None, :], w_pad, bias_pad, proj_pad, core.reshape(1)
    )
    tp_ways = lax.axis_size("tp")
    other = lax.ppermute(send, "tp", [(i, i ^ 1) for i in range(tp_ways)])
    chip_sum = (keep.astype(f32) + other.astype(f32)).astype(bf16)
    chips = tp_ways // 2
    take = lambda a, at: lax.dynamic_index_in_dim(a, at, 0, keepdims=False)
    arrived = [
        lax.ppermute(
            take(chip_sum, (chip + by) % chips), "tp", [(i, (i + 2 * by) % tp_ways) for i in range(tp_ways)]
        )
        for by in range(1, chips)
    ]
    half = width // 2
    cols = lambda a: lax.dynamic_slice_in_dim(a, core * half, half, a.ndim - 1)
    mixed = cols(take(window_rows, chip)).astype(f32) + cols(vis_proj_bias)
    for part in [take(chip_sum, chip)] + arrived:
        mixed = mixed + part.astype(f32)
    squares = jnp.sum(mixed * mixed, axis=-1).reshape(2, -1)
    squares = squares + lax.ppermute(squares, "tp", [(i, i ^ 1) for i in range(tp_ways)])
    factor = lax.rsqrt(squares.reshape(-1, 1) / width + EPS)
    merged = (mixed * factor * cols(merge_gain)).astype(bf16)
    requests = owner.shape[0]
    merged = merged.reshape(requests, -1, half)
    outgoing = place(owner, merged, groups)
    arrived = lax.all_to_all(outgoing, ("phase", "rep"), split_axis=0, concat_axis=0, tiled=True)
    image_buffer = place(image_at, arrived, groups).reshape(-1, half)

    rows, features = x.shape
    page_rows = rows // pages
    xf = x.astype(f32)
    row_factor = lax.rsqrt(jnp.mean(xf * xf, axis=-1, keepdims=True) + EPS)
    start = jnp.repeat(first_page, page_rows) * page_rows
    position = jnp.arange(rows, dtype=jnp.int32) - start
    half_dim = HD // 2
    inv_freq = jnp.exp(-jnp.log(1000000.0) * jnp.arange(half_dim).astype(f32) / half_dim)
    angles = position.astype(f32)[:, None] * inv_freq[None, :]
    cosine, sines = jnp.cos(angles), jnp.sin(angles)
    cosine = jnp.concatenate([cosine, cosine], axis=1)
    sines = jnp.concatenate([-sines, sines], axis=1)

    per = depth // LANE
    offset_of = lambda dp, dr: (((phase + dp) % n_phase) * n_rep + (rep + dr) % n_rep) * per
    offsets = []

    def unit(dp, dr, part=0, count=per):
        offsets.append(offset_of(dp, dr) + part)
        return (len(offsets) - 1, count)

    sides = [(0, [0, -1, 1, 2])]
    kv_units = []
    for dr in (0, -1, 1, -2, 2, -3, 3):
        kv_units.append([unit(dp, dr) for dp in (0, -1, 1, 2)])
    kv_units.append([unit(dp, 4) for dp in (0, -1)])
    kv_units.append([unit(dp, 4) for dp in (1, 2)])
    kv = kv_rows(
        jnp.stack(offsets).astype(jnp.int32), x, row_factor,
        jnp.concatenate([b_key, b_value])[None, :], cosine, sines, kv_pieces, kv_units,
    )
    kv_pages = kv.reshape(pages, page_rows, -1)
    outgoing_pages = place(owners * CAP + page_pos, kv_pages, n_rep * CAP)
    arrived_pages = lax.all_to_all(
        outgoing_pages.reshape(n_rep, CAP, page_rows, -1), "rep", split_axis=0, concat_axis=0, tiled=True
    )
    kv_pool = place(page_at, arrived_pages.reshape(n_rep * CAP, page_rows, -1), pages)

    offsets = []

    def span_units(dp, drs, low, high):
        out = []
        for index, dr in enumerate(drs):
            begin, end = max(low, index * per), min(high, (index + 1) * per)
            if begin < end:
                out.append(unit(dp, dr, begin - index * per, end - begin))
        return out

    pieces, units = [], []
    last = []
    for batch, drs in ((near, (0, -1, 1)), (far, (-2, 2, -3, 3, 4))):
        all_units = len(drs) * per
        for piece, dp in zip(batch[:3], (0, -1, 1)):
            pieces.append(piece)
            units.append(span_units(dp, drs, 0, all_units))
        ends = [(batch[3], 0, all_units // 2), (batch[4], all_units // 2, all_units)]
        for piece, low, high in ends:
            if batch is near:
                pieces.append(piece)
                units.append(span_units(2, drs, low, high))
            else:
                last += span_units(2, drs, low, high)
    sums, tail = query_sums(
        jnp.stack(offsets).astype(jnp.int32), x, pieces, units, last, 2 * far[3].shape[0]
    )
    attn_out = attend(
        sums, tail, far[3], far[4], row_factor, b_query[None, :], cosine, sines, start[:, None], kv
    )
    return (image_buffer, attn_out, kv_pool)


def solution(mesh):
    split, cut = P(("phase", "rep"), None), P(("phase", "rep"), "tp")
    return jax.shard_map(
        body,
        mesh=mesh,
        in_specs=(
            split, split, P(), P(None, "tp"), P("tp"), P("tp", None), P(), P(), split, split,
            cut, P(), cut, P("tp"), cut, P("tp"), cut, P("tp"), split, split,
        ),
        out_specs=(cut, cut, P(("phase", "rep"), None, "tp")),
        check_vma=False,
    )
```

```python
import jax
import jax.numpy as jnp
from jax import lax
from jax.experimental import pallas as pl
from jax.experimental.pallas import tpu as pltpu
from jax.sharding import PartitionSpec as P

VD = 1280
VHD = 80
LANE = 128
HD = 128
EPS = 1e-06
CAP = 5
UNIT = 256
LABEL_ROWS = 16
WINDOW = 384
VMEM_LIMIT = 56 * 1024 * 1024


def whole(shape):
    return pl.BlockSpec(shape, lambda *_: (0,) * len(shape))


def params(limit=VMEM_LIMIT):
    return pltpu.CompilerParams(vmem_limit_bytes=limit)


def shift(axis, by):
    n = lax.axis_size(axis)
    return lambda a: lax.ppermute(a, axis, [(i, (i + by) % n) for i in range(n)])


def spread_columns(count):
    shape = (count * VHD, count * LANE)
    source = lax.broadcasted_iota(jnp.int32, shape, 0)
    target = lax.broadcasted_iota(jnp.int32, shape, 1)
    inside = target & (LANE - 1)
    hit = (inside < VHD) & (source == (target >> 7) * VHD + inside)
    return jnp.where(hit, 1.0, 0.0).astype(jnp.bfloat16)


def spread_rows(count):
    shape = (count * LANE, count * VHD)
    target = lax.broadcasted_iota(jnp.int32, shape, 0)
    source = lax.broadcasted_iota(jnp.int32, shape, 1)
    inside = target & (LANE - 1)
    hit = (inside < VHD) & (source == (target >> 7) * VHD + inside)
    return jnp.where(hit, 1.0, 0.0).astype(jnp.bfloat16)


def vision_kernel(
    own_ref, order_ref, patches_ref, gain_ref, w_ref, bias_ref, proj_ref, keep_ref, send_ref,
    resid_ref, w_pad, proj_pad, held,
):
    parts, span, width = held.shape
    total = parts * span
    chunks = w_ref.shape[1] // VHD
    core, chip = own_ref[0], own_ref[1]

    @pl.when(pl.program_id(0) == 0)
    def _():
        w_pad[...] = jnp.dot(
            w_ref[...], spread_columns(chunks), preferred_element_type=jnp.float32
        ).astype(jnp.bfloat16)
        proj_pad[...] = jnp.dot(
            spread_rows(chunks // 3), proj_ref[...], preferred_element_type=jnp.float32
        ).astype(jnp.bfloat16)

    places = patches_ref.shape[0]
    wanted = order_ref[...].reshape(total, 1)
    onehot = jnp.where(
        wanted == lax.broadcasted_iota(jnp.int32, (total, places), 1), 1.0, 0.0
    ).astype(jnp.bfloat16)
    rows = jnp.dot(onehot, patches_ref[...], preferred_element_type=jnp.float32)
    held[...] = rows.astype(jnp.bfloat16).reshape(parts, span, width)
    half = width // 2
    mine = pl.multiple_of(core * half, LANE)
    other = pl.multiple_of((1 - core) * half, LANE)
    resid_ref[...] = held[chip, :, pl.ds(mine, half)]
    factor = lax.rsqrt(jnp.mean(rows * rows, axis=-1, keepdims=True) + EPS)
    normed = (rows * factor * gain_ref[...]).astype(jnp.bfloat16)
    projected = jnp.dot(normed, w_pad[...], preferred_element_type=jnp.float32) + bias_ref[...]
    projected = projected.astype(jnp.bfloat16)
    window_q = lax.broadcasted_iota(jnp.int32, (total, total), 0) % span // 16
    window_k = lax.broadcasted_iota(jnp.int32, (total, total), 1) % span // 16
    same = window_q == window_k
    heads = []
    for head in range(chunks // 3):
        at = head * 3 * LANE
        query = projected[:, at : at + LANE]
        keyed = projected[:, at + LANE : at + 2 * LANE]
        valued = projected[:, at + 2 * LANE : at + 3 * LANE]
        scores = lax.dot_general(
            query, keyed, (((1,), (1,)), ((), ())), preferred_element_type=jnp.float32
        ) * (VHD ** (-0.5))
        scores = jnp.where(same, scores, -1e30)
        raised = jnp.exp(scores - jnp.max(scores, axis=-1, keepdims=True))
        weights = (raised / jnp.sum(raised, axis=-1, keepdims=True)).astype(jnp.bfloat16)
        heads.append(
            jnp.dot(weights, valued, preferred_element_type=jnp.float32).astype(jnp.bfloat16)
        )
    mixed = jnp.concatenate(heads, axis=1)
    for out_ref, at in ((keep_ref, mine), (send_ref, other)):
        part = jnp.dot(mixed, proj_pad[:, pl.ds(at, half)], preferred_element_type=jnp.float32)
        out_ref[...] = part.astype(jnp.bfloat16).reshape(parts, span, half)


def vision_partial(order, patches, gain, w, bias_pad, proj, own):
    parts, span, _ = order.shape
    width = patches.shape[1]
    step = 64
    half = width // 2
    chunks = w.shape[1] // VHD
    spec = pl.BlockSpec((parts, step, half), lambda i, _: (0, i, 0))
    out = jax.ShapeDtypeStruct((parts, span, half), jnp.bfloat16)
    return pl.pallas_call(
        vision_kernel,
        grid_spec=pltpu.PrefetchScalarGridSpec(
            num_scalar_prefetch=1,
            grid=(span // step,),
            in_specs=[
                pl.BlockSpec((parts, step, 1), lambda i, _: (0, i, 0)),
                whole(patches.shape),
                whole(gain.shape),
                whole(w.shape),
                whole(bias_pad.shape),
                whole(proj.shape),
            ],
            out_specs=[spec, spec, pl.BlockSpec((step, half), lambda i, _: (i, 0))],
            scratch_shapes=[
                pltpu.VMEM((width, chunks * LANE), jnp.bfloat16),
                pltpu.VMEM((chunks // 3 * LANE, width), jnp.bfloat16),
                pltpu.VMEM((parts, step, width), jnp.bfloat16),
            ],
        ),
        out_shape=[out, out, jax.ShapeDtypeStruct((span, half), jnp.bfloat16)],
        compiler_params=params(),
        cost_estimate=pl.CostEstimate(
            flops=10_000_000_000, bytes_accessed=8_000_000, transcendentals=0
        ),
    )(own, order, patches, gain, w, bias_pad, proj)


def join_kernel(*refs):
    out_ref = refs[-1]
    at = 0
    for ref in refs[:-1]:
        out_ref[at : at + ref.shape[0]] = ref[...]
        at += ref.shape[0]


def join(*parts):
    shape = (sum(part.shape[0] for part in parts),) + parts[0].shape[1:]
    return pl.pallas_call(
        join_kernel,
        grid=(1,),
        in_specs=[whole(part.shape) for part in parts],
        out_specs=whole(shape),
        out_shape=jax.ShapeDtypeStruct(shape, parts[0].dtype),
        compiler_params=params(),
    )(*parts)


def scale_kernel(gain_ref, query_ref, key_ref, value_ref, label_ref, own_ref, own_kv_ref):
    gain = gain_ref[...]
    scaled = lambda ref: (ref[...].astype(jnp.float32) * gain).astype(jnp.bfloat16)
    own_ref[...] = scaled(query_ref)
    depth, width = key_ref.shape
    own_kv_ref[:depth, :width] = scaled(key_ref)
    own_kv_ref[:depth, width:] = scaled(value_ref)
    own_kv_ref[depth:, :] = jnp.broadcast_to(label_ref[...], (LABEL_ROWS, 2 * width))


def scale(gain, w_query, w_key, w_value, label):
    depth, width = w_key.shape
    shapes = [w_query.shape, (depth + LABEL_ROWS, 2 * width)]
    return pl.pallas_call(
        scale_kernel,
        grid=(1,),
        in_specs=[whole(a.shape) for a in (gain, w_query, w_key, w_value, label)],
        out_specs=[whole(shape) for shape in shapes],
        out_shape=[jax.ShapeDtypeStruct(shape, jnp.bfloat16) for shape in shapes],
        compiler_params=params(),
    )(gain, w_query, w_key, w_value, label)


def place_kernel(at_ref, from_ref, items_ref, out_ref):
    out_ref[...] = jnp.zeros_like(out_ref)
    for index in range(at_ref.shape[0]):
        at = at_ref[index]

        @pl.when(at >= 0)
        def _():
            out_ref[pl.ds(at, 1)] = items_ref[pl.ds(from_ref[index], 1)]


def place(at, source, items, slots):
    shape = (slots,) + items.shape[1:]
    return pl.pallas_call(
        place_kernel,
        grid_spec=pltpu.PrefetchScalarGridSpec(
            num_scalar_prefetch=2,
            grid=(1,),
            in_specs=[whole(items.shape)],
            out_specs=whole(shape),
        ),
        out_shape=jax.ShapeDtypeStruct(shape, items.dtype),
        compiler_params=params(),
    )(at, source, items)


def assemble(ways_ref, x_refs, held):
    width = x_refs[0].shape[1]
    for index, x_ref in enumerate(x_refs):
        held[:, pl.ds(pl.multiple_of(ways_ref[index] * width, LANE), width)] = x_ref[...]


def columns(held, offsets_ref, units):
    return jnp.concatenate(
        [
            held[:, pl.ds(pl.multiple_of(offsets_ref[unit] * UNIT, LANE), UNIT)]
            for unit in units
        ],
        axis=1,
    )


def rotary(values, cosine, sines):
    return values * cosine + pltpu.roll(values, HD // 2, 1) * sines


def kv_kernel(
    ways_ref, offsets_ref, dest_ref, *refs,
):
    x_refs = refs[:8]
    w_ref, bias_ref, cos_ref, sin_ref, out_ref, pages_ref, factor_ref, label_ref, held = refs[8:]
    step, depth = held.shape
    assemble(ways_ref, x_refs, held)
    squares = jnp.zeros((step, 1), jnp.float32)
    for at in range(0, depth, 1024):
        part = held[:, at : at + 1024].astype(jnp.float32)
        squares += jnp.sum(part * part, axis=-1, keepdims=True)
    factor = lax.rsqrt(squares / depth + EPS)
    factor_ref[...] = factor
    total = jnp.zeros((step, w_ref.shape[1]), jnp.float32)
    span = UNIT + LABEL_ROWS
    for index in range(depth // UNIT):
        total += jnp.dot(
            held[:, pl.ds(pl.multiple_of(offsets_ref[index] * UNIT, LANE), UNIT)],
            w_ref[index * span : index * span + UNIT, :],
            preferred_element_type=jnp.float32,
        )
        label_ref[index : index + 1, :] = w_ref[
            index * span + UNIT : index * span + UNIT + 16, :LANE
        ][:1].astype(jnp.float32)
    total = total * factor + bias_ref[...]
    keyed = rotary(total[:, :HD], cos_ref[...], sin_ref[...]).astype(jnp.bfloat16)
    out_ref[:, :HD] = keyed
    out_ref[:, HD:] = total[:, HD:].astype(jnp.bfloat16)
    block = pl.program_id(0)

    @pl.when(block == 0)
    def _():
        pages_ref[...] = jnp.zeros_like(pages_ref)

    rows = pages_ref.shape[1]
    for page in range(step // rows):
        at = dest_ref[block * (step // rows) + page]
        pages_ref[pl.ds(at, 1)] = out_ref[page * rows : (page + 1) * rows, :][None]


def kv_rows(ways, offsets, dest, xs, w, bias, cosine, sines, slots, page_rows):
    rows, part = xs[0].shape
    step = 256
    by_rows = lambda width: pl.BlockSpec((step, width), lambda i, *_: (i, 0))
    width = w.shape[1]
    depth = part * len(xs)
    pages = (slots, page_rows, width)
    labels = (depth // UNIT, LANE)
    return pl.pallas_call(
        kv_kernel,
        grid_spec=pltpu.PrefetchScalarGridSpec(
            num_scalar_prefetch=3,
            grid=(rows // step,),
            in_specs=[by_rows(part)] * len(xs)
            + [whole(w.shape), whole(bias.shape), by_rows(HD), by_rows(HD)],
            out_specs=[by_rows(width), whole(pages), by_rows(1), whole(labels)],
            scratch_shapes=[pltpu.VMEM((step, depth), jnp.bfloat16)],
        ),
        out_shape=[
            jax.ShapeDtypeStruct((rows, width), jnp.bfloat16),
            jax.ShapeDtypeStruct(pages, jnp.bfloat16),
            jax.ShapeDtypeStruct((rows, 1), jnp.float32),
            jax.ShapeDtypeStruct(labels, jnp.float32),
        ],
        compiler_params=params(),
        cost_estimate=pl.CostEstimate(
            flops=2 * rows * depth * width, bytes_accessed=13_000_000, transcendentals=0
        ),
    )(ways, offsets, dest, *xs, w, bias, cosine, sines)


def query_kernel(units, tail_units, ways_ref, offsets_ref, *refs):
    x_refs, pieces = refs[:8], refs[8:-3]
    out_ref, tail_ref, held = refs[-3:]
    assemble(ways_ref, x_refs, held)
    total = jnp.zeros(out_ref.shape, jnp.float32)
    for piece_ref, own in zip(pieces, units):
        total += jnp.dot(
            columns(held, offsets_ref, own), piece_ref[...], preferred_element_type=jnp.float32
        )
    out_ref[...] = total
    tail_ref[...] = columns(held, offsets_ref, tail_units)


def query_sums(ways, offsets, xs, pieces, units, tail_units):
    rows, part = xs[0].shape
    step = 256
    by_rows = lambda width: pl.BlockSpec((step, width), lambda i, *_: (i, 0))
    width = pieces[0].shape[1]
    depth = part * len(xs)
    tail_width = len(tail_units) * UNIT
    return pl.pallas_call(
        lambda *refs: query_kernel(units, tail_units, *refs),
        grid_spec=pltpu.PrefetchScalarGridSpec(
            num_scalar_prefetch=2,
            grid=(rows // step,),
            in_specs=[by_rows(part)] * len(xs) + [whole(piece.shape) for piece in pieces],
            out_specs=[by_rows(width), by_rows(tail_width)],
            scratch_shapes=[pltpu.VMEM((step, depth), jnp.bfloat16)],
        ),
        out_shape=[
            jax.ShapeDtypeStruct((rows, width), jnp.float32),
            jax.ShapeDtypeStruct((rows, tail_width), jnp.bfloat16),
        ],
        compiler_params=params(),
        cost_estimate=pl.CostEstimate(
            flops=2 * rows * depth * width, bytes_accessed=18_000_000, transcendentals=0
        ),
    )(ways, offsets, *xs, *pieces)


def attend_kernel(
    sums_ref, tail_ref, last_ref, factor_ref, bias_ref, cos_ref, sin_ref, start_ref, kv_ref, out_ref,
):
    step = sums_ref.shape[0]
    block = pl.program_id(0)
    total = sums_ref[...] + jnp.dot(
        tail_ref[...], last_ref[...], preferred_element_type=jnp.float32
    )
    total = total * factor_ref[...] + bias_ref[...]
    heads = total.shape[1] // HD
    query = jnp.concatenate(
        [
            rotary(total[:, h * HD : (h + 1) * HD], cos_ref[...], sin_ref[...]).astype(jnp.bfloat16)
            for h in range(heads)
        ],
        axis=0,
    )
    begin = pl.multiple_of(jnp.maximum(block * step + step - WINDOW, 0), LANE)
    keyed = kv_ref[pl.ds(begin, WINDOW), :HD]
    valued = kv_ref[pl.ds(begin, WINDOW), HD:]
    scores = lax.dot_general(
        query, keyed, (((1,), (1,)), ((), ())), preferred_element_type=jnp.float32
    ) * (HD ** (-0.5))
    key_at = begin + lax.broadcasted_iota(jnp.int32, (step, WINDOW), 1)
    row_at = block * step + lax.broadcasted_iota(jnp.int32, (step, WINDOW), 0)
    allowed = (key_at <= row_at) & (key_at >= start_ref[...])
    for h in range(heads):
        own = jnp.where(allowed, scores[h * step : (h + 1) * step], -1e30)
        raised = jnp.exp(own - jnp.max(own, axis=-1, keepdims=True))
        weights = (raised / jnp.sum(raised, axis=-1, keepdims=True)).astype(jnp.bfloat16)
        mixed = jnp.dot(weights, valued, preferred_element_type=jnp.float32)
        out_ref[:, h * HD : (h + 1) * HD] = mixed.astype(jnp.bfloat16)


def attend(sums, tail, last, factor, bias, cosine, sines, start, kv):
    rows, width = sums.shape
    step = 256
    by_rows = lambda cols: pl.BlockSpec((step, cols), lambda i: (i, 0))
    return pl.pallas_call(
        attend_kernel,
        grid=(rows // step,),
        in_specs=[
            by_rows(width),
            by_rows(tail.shape[1]),
            whole(last.shape),
            by_rows(1),
            whole(bias.shape),
            by_rows(HD),
            by_rows(HD),
            by_rows(1),
            whole(kv.shape),
        ],
        out_specs=by_rows(width),
        out_shape=jax.ShapeDtypeStruct((rows, width), jnp.bfloat16),
        compiler_params=params(),
    )(sums, tail, last, factor, bias, cosine, sines, start, kv)


def after(values, *others):
    return lax.optimization_barrier((tuple(values),) + others)[0]


def body(
    patches, window_order, vis_gain, vis_qkv, vis_qkv_bias, vis_proj, vis_proj_bias, merge_gain,
    img_owner, img_slot, prompt_rows, lang_gain, w_query, b_query, w_key, b_key, w_value, b_value,
    page_owner, page_slot,
):
    phase, rep, tp = lax.axis_index("phase"), lax.axis_index("rep"), lax.axis_index("tp")
    n_phase, n_rep = lax.axis_size("phase"), lax.axis_size("rep")
    groups = n_phase * n_rep
    group = phase * n_rep + rep
    chip, core = tp // 2, tp % 2
    bf16, f32 = jnp.bfloat16, jnp.float32

    up, down = shift("rep", 1), shift("rep", -1)
    fore, back = shift("phase", 1), shift("phase", -1)
    tp_ways = lax.axis_size("tp")
    chips = tp_ways // 2
    across = lambda a, by: lax.ppermute(
        a, "tp", [(i, (i + 2 * by) % tp_ways) for i in range(tp_ways)]
    )
    partner = lambda a: lax.ppermute(a, "tp", [(i, i ^ 1) for i in range(tp_ways)])
    take = lambda a, at: lax.dynamic_index_in_dim(a, at, 0, keepdims=False)

    owner, owners = img_owner[0], page_owner[0]
    label = jnp.concatenate([owner, img_slot[0], owners, page_slot[0]]).astype(bf16)
    label = jnp.pad(label, (0, 2 * w_key.shape[1] - label.shape[0]))[None, :]

    depth = w_query.shape[0]
    gain = lax.dynamic_slice_in_dim(lang_gain, group * depth, depth)[:, None]
    own, own_kv = scale(gain, w_query, w_key, w_value, label)

    kv_all = (own_kv, fore(own_kv), back(own_kv), shift("phase", 2)(own_kv))
    up1, down1 = up(own), down(own)
    x_chips = [prompt_rows] + [across(prompt_rows, by) for by in (1, -1, 2)]

    pages = owners.shape[0]
    rows = prompt_rows.shape[0]
    page_rows = rows // pages
    page_iota = jnp.arange(pages, dtype=jnp.int32)
    first_of = lambda ids: jnp.min(
        jnp.where(ids[..., :, None] == ids[..., None, :], page_iota, pages), axis=-1
    )
    first_page = first_of(owners)
    start = jnp.repeat(first_page, page_rows) * page_rows
    position = jnp.arange(rows, dtype=jnp.int32) - start
    half_dim = HD // 2
    inv_freq = jnp.exp(-jnp.log(1000000.0) * jnp.arange(half_dim).astype(f32) / half_dim)
    angles = position.astype(f32)[:, None] * inv_freq[None, :]
    cosine, sines = jnp.cos(angles), jnp.sin(angles)
    cosine = jnp.concatenate([cosine, cosine], axis=1)
    sines = jnp.concatenate([-sines, sines], axis=1)
    patch_count, width = patches.shape
    merge = 4
    order = window_order[0].reshape(patch_count // merge, merge).T[:, :, None]
    chunks = vis_qkv.shape[1] // VHD
    bias_pad = jnp.pad(vis_qkv_bias.reshape(chunks, VHD), ((0, 0), (0, LANE - VHD))).reshape(1, -1)
    order, bias_pad, cosine, sines, up1, down1, *kv_all = after(
        (order, bias_pad, cosine, sines, up1, down1, *kv_all)
    )

    kv_weights = lax.all_gather(join(*kv_all), "rep", axis=0, tiled=True)
    up2, down2 = up(up1), down(down1)
    near = join(own, up1, down1)
    near_fore, near_back = fore(near), back(near)
    keep, send, resid = vision_partial(
        order, patches, vis_gain[None, :], vis_qkv, bias_pad, vis_proj, jnp.stack([core, chip])
    )
    keep, send, up2, down2 = after((keep, send, up2, down2))

    up3, down3 = up(up2), down(down2)
    chip_sum = (keep.astype(f32) + partner(send).astype(f32)).astype(bf16)
    chip_sum, up3, down3, near_fore, near_back = after(
        (chip_sum, up3, down3, near_fore, near_back)
    )

    up4 = up(up3)
    near_two = fore(near_fore)
    arrived = [across(take(chip_sum, (chip + by) % chips), by) for by in (1, -1, 2)]
    far = join(up2, down2, up3, down3, up4)
    far_fore, far_back = fore(far), back(far)
    x_chips = list(after((*x_chips, up4)))[:4]
    xs = x_chips + [partner(a) for a in x_chips]

    half = width // 2
    cols = lambda a: lax.dynamic_slice_in_dim(a, core * half, half, a.ndim - 1)
    mixed = resid.astype(f32) + cols(vis_proj_bias)
    for part in [take(chip_sum, chip)] + arrived:
        mixed = mixed + part.astype(f32)
    squares = jnp.sum(mixed * mixed, axis=-1).reshape(2, -1)
    squares = squares + partner(squares)
    factor = lax.rsqrt(squares.reshape(-1, 1) / width + EPS)
    merged = (mixed * factor * cols(merge_gain)).astype(bf16)
    requests = owner.shape[0]
    merged = merged.reshape(requests, -1, half)
    outgoing = place(owner, jnp.arange(requests, dtype=jnp.int32), merged, groups)
    images = lax.all_to_all(outgoing, ("phase", "rep"), split_axis=0, concat_axis=0, tiled=True)

    ways = jnp.stack(
        [((chip - by) % chips) * 2 + side for side in (core, 1 - core) for by in (0, 1, -1, 2)]
    ).astype(jnp.int32)
    hops = (0, -1, 1, 2)
    offset_of = lambda dp, at: ((phase + dp) % n_phase) * n_rep + at % n_rep
    kv_offsets = jnp.stack([offset_of(dp, at) for at in range(n_rep) for dp in hops])
    kv, outgoing_pages, row_factor, labels = kv_rows(
        ways, kv_offsets.astype(jnp.int32), owners * CAP + page_iota - first_page, xs, kv_weights,
        jnp.concatenate([b_key, b_value])[None, :], cosine, sines, n_rep * CAP, page_rows,
    )
    arrived_pages = lax.all_to_all(
        outgoing_pages.reshape(n_rep, CAP, page_rows, -1), "rep", split_axis=0, concat_axis=0, tiled=True
    )

    labels = labels[:, : 4 * requests].astype(jnp.int32).reshape(n_rep, n_phase, 4, -1)
    image_at = jnp.sum(
        jnp.where(labels[:, :, 0] == group, labels[:, :, 1] + 1, 0), axis=-1
    ).reshape(-1) - 1
    page_at = jnp.where(labels[:, 0, 2] == rep, labels[:, 0, 3], -1).reshape(-1)
    page_from = (
        jnp.arange(n_rep, dtype=jnp.int32)[:, None] * CAP + page_iota - first_of(labels[:, 0, 2])
    ).reshape(-1)
    image_buffer = place(image_at, kv_offsets.astype(jnp.int32), images, groups).reshape(-1, half)
    kv_pool = place(page_at, page_from, arrived_pages.reshape(n_rep * CAP, page_rows, -1), pages)

    far_fore, far_back, near_two = after((far_fore, far_back, near_two))
    far_two = back(far_back)
    offsets, pieces, units = [], [], []

    def units_of(dp, drs):
        at = len(offsets)
        offsets.extend(offset_of(dp, rep + dr) for dr in drs)
        return list(range(at, at + len(drs)))

    near_reps, far_reps = (0, -1, 1), (-2, 2, -3, 3, -4)
    for piece, dp, reps in (
        (near, 0, near_reps), (near_fore, -1, near_reps), (near_back, 1, near_reps),
        (near_two, 2, near_reps), (far, 0, far_reps), (far_fore, -1, far_reps),
        (far_back, 1, far_reps),
    ):
        pieces.append(piece)
        units.append(units_of(dp, reps))
    last = units_of(2, far_reps)
    sums, tail = query_sums(ways, jnp.stack(offsets).astype(jnp.int32), xs, pieces, units, last)
    attn_out = attend(
        sums, tail, far_two, row_factor, b_query[None, :], cosine, sines, start[:, None], kv
    )
    return (image_buffer, attn_out, kv_pool)


def solution(mesh):
    split, cut = P(("phase", "rep"), None), P(("phase", "rep"), "tp")
    return jax.shard_map(
        body,
        mesh=mesh,
        in_specs=(
            split, split, P(), P(None, "tp"), P("tp"), P("tp", None), P(), P(), split, split,
            cut, P(), cut, P("tp"), cut, P("tp"), cut, P("tp"), split, split,
        ),
        out_specs=(cut, cut, P(("phase", "rep"), None, "tp")),
        check_vma=False,
    )
```

```python
import jax
import jax.numpy as jnp
from jax import lax
from jax.experimental import pallas as pl
from jax.experimental.pallas import tpu as pltpu
from jax.sharding import PartitionSpec as P

VD = 1280
VHD = 80
LANE = 128
HD = 128
EPS = 1e-06
CAP = 5
AHEAD = 3
WINDOW = 384
VMEM_LIMIT = 58 * 1024 * 1024


def resident():
    return pl.BlockSpec(memory_space=pltpu.VMEM)


def whole(shape):
    return pl.BlockSpec(shape, lambda *_: (0,) * len(shape))


def params(limit=VMEM_LIMIT):
    return pltpu.CompilerParams(vmem_limit_bytes=limit)


def cheap():
    return pl.CostEstimate(flops=1_000_000, bytes_accessed=1000, transcendentals=0)


def vision_kernel(own_ref, order_ref, patches_ref, gain_ref, w_ref, bias_ref, proj_ref, *refs):
    keep_ref, send_ref, resid_ref, w_pad, proj_pad, held, apart = refs[-7:]
    parts, span, width = held.shape
    total = parts * span
    chunks = w_ref.shape[0] // VHD
    core, chip = own_ref[0], own_ref[1]

    @pl.when(pl.program_id(0) == 0)
    def _():
        w_pad[...] = jnp.zeros_like(w_pad)
        proj_pad[...] = jnp.zeros_like(proj_pad)
        for pad, ref in ((w_pad, w_ref), (proj_pad, proj_ref)):
            for at in range(ref.shape[0] // VHD):
                pad[at * LANE : at * LANE + VHD] = ref[at * VHD : (at + 1) * VHD]
        window_q = (lax.broadcasted_iota(jnp.int32, (total, total), 0) & (span - 1)) >> 4
        window_k = (lax.broadcasted_iota(jnp.int32, (total, total), 1) & (span - 1)) >> 4
        apart[...] = jnp.where(window_q == window_k, 0.0, -1e30)

    places = patches_ref.shape[0]
    wanted = order_ref[...].reshape(total, 1)
    onehot = jnp.where(
        wanted == lax.broadcasted_iota(jnp.int32, (total, places), 1), 1.0, 0.0
    ).astype(jnp.bfloat16)
    rows = jnp.dot(onehot, patches_ref[...], preferred_element_type=jnp.float32)
    held[...] = rows.astype(jnp.bfloat16).reshape(parts, span, width)
    half = width // 2
    mine = pl.multiple_of(core * half, LANE)
    other = pl.multiple_of((1 - core) * half, LANE)
    resid_ref[...] = held[chip, :, pl.ds(mine, half)]
    factor = lax.rsqrt(jnp.mean(rows * rows, axis=-1, keepdims=True) + EPS)
    normed = (rows * factor * gain_ref[...][None, :]).astype(jnp.bfloat16)
    projected = lax.dot_general(
        normed, w_pad[...], (((1,), (1,)), ((), ())), preferred_element_type=jnp.float32
    )
    projected = (projected + bias_ref[...]).astype(jnp.bfloat16)
    heads = []
    for head in range(chunks // 3):
        at = head * 3 * LANE
        query = projected[:, at : at + LANE]
        keyed = projected[:, at + LANE : at + 2 * LANE]
        valued = projected[:, at + 2 * LANE : at + 3 * LANE]
        scores = lax.dot_general(
            query, keyed, (((1,), (1,)), ((), ())), preferred_element_type=jnp.float32
        )
        scores = scores * (VHD ** (-0.5)) + apart[...]
        raised = jnp.exp(scores - jnp.max(scores, axis=-1, keepdims=True))
        scale_back = 1.0 / jnp.sum(raised, axis=-1, keepdims=True)
        weights = raised.astype(jnp.bfloat16)
        mixed = jnp.dot(weights, valued, preferred_element_type=jnp.float32) * scale_back
        heads.append(mixed.astype(jnp.bfloat16))
    mixed = jnp.concatenate(heads, axis=1)
    for out_ref, at in ((keep_ref, mine), (send_ref, other)):
        part = jnp.dot(mixed, proj_pad[:, pl.ds(at, half)], preferred_element_type=jnp.float32)
        out_ref[...] = part.astype(jnp.bfloat16).reshape(parts, span, half)


def vision_partial(order, patches, gain, w, bias_pad, proj, own):
    parts, span, _ = order.shape
    width = patches.shape[1]
    step = 64
    half = width // 2
    chunks = w.shape[0] // VHD
    spec = pl.BlockSpec((parts, step, half), lambda i, _: (0, i, 0))
    out = jax.ShapeDtypeStruct((parts, span, half), jnp.bfloat16)
    return pl.pallas_call(
        vision_kernel,
        grid_spec=pltpu.PrefetchScalarGridSpec(
            num_scalar_prefetch=1,
            grid=(span // step,),
            in_specs=[
                pl.BlockSpec((parts, step, 1), lambda i, _: (0, i, 0)),
                whole(patches.shape),
                whole(gain.shape),
                whole(w.shape),
                whole(bias_pad.shape),
                whole(proj.shape),
            ],
            out_specs=[spec, spec, pl.BlockSpec((step, half), lambda i, _: (i, 0))],
            scratch_shapes=[
                pltpu.VMEM((chunks * LANE, width), jnp.bfloat16),
                pltpu.VMEM((chunks // 3 * LANE, width), jnp.bfloat16),
                pltpu.VMEM((parts, step, width), jnp.bfloat16),
                pltpu.VMEM((parts * step, parts * step), jnp.float32),
            ],
        ),
        out_shape=[out, out, jax.ShapeDtypeStruct((span, half), jnp.bfloat16)],
        compiler_params=params(),
        cost_estimate=pl.CostEstimate(
            flops=14_000_000_000, bytes_accessed=6_000_000, transcendentals=0
        ),
    )(own, order, patches, gain, w, bias_pad, proj)


def join_kernel(*refs):
    out_ref = refs[-1]
    at = 0
    for ref in refs[:-1]:
        out_ref[at : at + ref.shape[0]] = ref[...]
        at += ref.shape[0]


def join(*parts):
    shape = (sum(part.shape[0] for part in parts),) + parts[0].shape[1:]
    return pl.pallas_call(
        join_kernel,
        grid=(1,),
        in_specs=[whole(part.shape) for part in parts],
        out_specs=whole(shape),
        out_shape=jax.ShapeDtypeStruct(shape, parts[0].dtype),
        compiler_params=params(),
    )(*parts)


def scale_kernel(gain_ref, query_ref, key_ref, value_ref, out_ref):
    gain = gain_ref[...]
    at = 0
    for ref in (key_ref, value_ref, query_ref):
        width = ref.shape[1]
        scaled = ref[...].astype(jnp.float32) * gain
        out_ref[:, at : at + width] = scaled.astype(jnp.bfloat16)
        at += width


def scale(gain, w_query, w_key, w_value):
    parts = (gain, w_query, w_key, w_value)
    shape = (w_query.shape[0], sum(part.shape[1] for part in parts[1:]))
    return pl.pallas_call(
        scale_kernel,
        grid=(1,),
        in_specs=[whole(part.shape) for part in parts],
        out_specs=whole(shape),
        out_shape=jax.ShapeDtypeStruct(shape, jnp.bfloat16),
        compiler_params=params(),
    )(*parts)


def place_kernel(at_ref, items_ref, out_ref):
    out_ref[...] = jnp.zeros_like(out_ref)
    for index in range(items_ref.shape[0]):
        at = at_ref[index]

        @pl.when(at >= 0)
        def _():
            out_ref[pl.ds(at, 1)] = items_ref[index : index + 1]


def place(at, items, slots):
    shape = (slots,) + items.shape[1:]
    return pl.pallas_call(
        place_kernel,
        grid_spec=pltpu.PrefetchScalarGridSpec(
            num_scalar_prefetch=1,
            grid=(1,),
            in_specs=[whole(items.shape)],
            out_specs=whole(shape),
        ),
        out_shape=jax.ShapeDtypeStruct(shape, items.dtype),
        compiler_params=params(),
    )(at, items)


def rotary(values, cosine, sines):
    return values * cosine + pltpu.roll(values, HD // 2, 1) * sines


def anywhere():
    return pl.BlockSpec(memory_space=pl.ANY)


def order_kernel(ways_ref, *refs):
    x_refs, (out_ref, factor_ref, held, sems) = refs[:-4], refs[-4:]
    parts, rows, part = held.shape
    each = parts // len(x_refs)
    loads, stores = [], []
    for index in range(parts):
        at = index % each * rows
        source = x_refs[index // each].at[at : at + rows]
        loads.append(pltpu.make_async_copy(source, held.at[index], sems.at[index]))
        stores.append(
            pltpu.make_async_copy(
                held.at[index], out_ref.at[ways_ref[index]], sems.at[parts + index]
            )
        )
    for load in loads[:AHEAD]:
        load.start()
    squares = jnp.zeros((rows, LANE), jnp.float32)
    for index in range(parts):
        loads[index].wait()
        stores[index].start()
        for load in loads[index + AHEAD : index + AHEAD + 1]:
            load.start()
        for at in range(0, part, LANE):
            wide = held[index, :, at : at + LANE].astype(jnp.float32)
            squares += wide * wide
    squares = jnp.sum(squares, axis=-1, keepdims=True)
    factor_ref[...] = lax.rsqrt(squares / (parts * part) + EPS)
    for store in stores:
        store.wait()


def ordered(ways, rows, xs):
    parts, part = ways.shape[0], xs[0].shape[1]
    return pl.pallas_call(
        order_kernel,
        in_specs=[pl.BlockSpec(memory_space=pltpu.SMEM)] + [anywhere()] * len(xs),
        out_specs=[anywhere(), resident()],
        out_shape=[
            jax.ShapeDtypeStruct((parts, rows, part), jnp.bfloat16),
            jax.ShapeDtypeStruct((rows, 1), jnp.float32),
        ],
        scratch_shapes=[
            pltpu.VMEM((parts, rows, part), jnp.bfloat16),
            pltpu.SemaphoreType.DMA((2 * parts,)),
        ],
        compiler_params=params(),
        cost_estimate=cheap(),
    )(ways, *xs)


def kv_kernel(dest_ref, x_ref, w_ref, *refs):
    factor_ref, bias_ref, cos_ref, sin_ref, out_ref, pages_ref = refs[:6]
    x_held, held, sems = refs[6:]
    parts, rows, part = x_held.shape
    width = held.shape[2]
    loads = []
    for i in range(parts):
        rows_of = w_ref.at[i * part : (i + 1) * part, :width]
        loads.append(pltpu.make_async_copy(x_ref.at[i], x_held.at[i], sems.at[2 * i]))
        loads.append(pltpu.make_async_copy(rows_of, held.at[i], sems.at[2 * i + 1]))
    for copy in loads[: 2 * AHEAD]:
        copy.start()
    pages_ref[...] = jnp.zeros_like(pages_ref)
    total = jnp.zeros(out_ref.shape, jnp.float32)
    for index in range(parts):
        loads[2 * index].wait()
        loads[2 * index + 1].wait()
        for copy in loads[2 * (index + AHEAD) : 2 * (index + AHEAD + 1)]:
            copy.start()
        total += jnp.dot(x_held[index], held[index], preferred_element_type=jnp.float32)
    total = total * factor_ref[...] + bias_ref[...]
    out_ref[:, :HD] = rotary(total[:, :HD], cos_ref[...], sin_ref[...]).astype(jnp.bfloat16)
    out_ref[:, HD:] = total[:, HD:].astype(jnp.bfloat16)
    page_rows = pages_ref.shape[1]
    for page in range(rows // page_rows):
        pages_ref[pl.ds(dest_ref[page], 1)] = out_ref[
            page * page_rows : (page + 1) * page_rows, :
        ][None]


def kv_rows(dest, x, w, factor, bias, cosine, sines, slots, page_rows):
    parts, rows, part = x.shape
    width = bias.shape[1]
    small = (factor, bias, cosine, sines)
    shapes = [(rows, width), (slots, page_rows, width)]
    return pl.pallas_call(
        kv_kernel,
        in_specs=[pl.BlockSpec(memory_space=pltpu.SMEM)]
        + [anywhere()] * 2
        + [resident()] * len(small),
        out_specs=[resident()] * 2,
        out_shape=[jax.ShapeDtypeStruct(shape, jnp.bfloat16) for shape in shapes],
        scratch_shapes=[
            pltpu.VMEM(x.shape, jnp.bfloat16),
            pltpu.VMEM((parts, part, width), jnp.bfloat16),
            pltpu.SemaphoreType.DMA((2 * parts,)),
        ],
        compiler_params=params(),
        cost_estimate=pl.CostEstimate(
            flops=7_000_000_000, bytes_accessed=13_000_000, transcendentals=0
        ),
    )(dest, x, w, *small)


def attend_kernel(x_ref, w_ref, *refs):
    factor_ref, bias_ref, cos_ref, sin_ref, start_ref, kv_ref, out_ref = refs[:7]
    x_held, held, sems = refs[7:]
    parts, rows, part = x_held.shape
    skip = w_ref.shape[1] - held.shape[2]
    loads = []
    for i in range(parts):
        rows_of = w_ref.at[i * part : (i + 1) * part, skip:]
        loads.append(pltpu.make_async_copy(x_ref.at[i], x_held.at[i], sems.at[2 * i]))
        loads.append(pltpu.make_async_copy(rows_of, held.at[i], sems.at[2 * i + 1]))
    for copy in loads[: 2 * AHEAD]:
        copy.start()
    total = jnp.zeros(out_ref.shape, jnp.float32)
    for index in range(parts):
        loads[2 * index].wait()
        loads[2 * index + 1].wait()
        for copy in loads[2 * (index + AHEAD) : 2 * (index + AHEAD + 1)]:
            copy.start()
        total += jnp.dot(x_held[index], held[index], preferred_element_type=jnp.float32)
    total = total * factor_ref[...] + bias_ref[...]
    step = 256
    for first in range(0, rows, step):
        span = slice(first, first + step)
        begin = max(first + step - WINDOW, 0)
        end = first + step
        keyed = kv_ref[begin:end, :HD]
        valued = kv_ref[begin:end, HD:]
        key_at = begin + lax.broadcasted_iota(jnp.int32, (step, end - begin), 1)
        row_at = first + lax.broadcasted_iota(jnp.int32, (step, end - begin), 0)
        allowed = (key_at <= row_at) & (key_at >= start_ref[span, :])
        cosine, sines = cos_ref[span, :], sin_ref[span, :]
        for at in range(0, total.shape[1], HD):
            query = rotary(total[span, at : at + HD], cosine, sines).astype(jnp.bfloat16)
            scores = lax.dot_general(
                query, keyed, (((1,), (1,)), ((), ())), preferred_element_type=jnp.float32
            ) * (HD ** (-0.5))
            scores = jnp.where(allowed, scores, -1e30)
            raised = jnp.exp(scores - jnp.max(scores, axis=-1, keepdims=True))
            scale_back = 1.0 / jnp.sum(raised, axis=-1, keepdims=True)
            weights = raised.astype(jnp.bfloat16)
            mixed = jnp.dot(weights, valued, preferred_element_type=jnp.float32) * scale_back
            out_ref[span, at : at + HD] = mixed.astype(jnp.bfloat16)


def attend(x, w, factor, bias, cosine, sines, start, kv):
    parts, rows, part = x.shape
    width = bias.shape[1]
    small = (factor, bias, cosine, sines, start, kv)
    return pl.pallas_call(
        attend_kernel,
        in_specs=[anywhere()] * 2 + [resident()] * len(small),
        out_specs=resident(),
        out_shape=jax.ShapeDtypeStruct((rows, width), jnp.bfloat16),
        scratch_shapes=[
            pltpu.VMEM(x.shape, jnp.bfloat16),
            pltpu.VMEM((parts, part, width), jnp.bfloat16),
            pltpu.SemaphoreType.DMA((2 * parts,)),
        ],
        compiler_params=params(),
        cost_estimate=pl.CostEstimate(
            flops=14_000_000_000, bytes_accessed=17_000_000, transcendentals=0
        ),
    )(x, w, *small)


def after(values, *others):
    return lax.optimization_barrier((tuple(values),) + others)[0]


def body(
    patches, window_order, vis_gain, vis_qkv, vis_qkv_bias, vis_proj, vis_proj_bias, merge_gain,
    img_owner, img_slot, prompt_rows, lang_gain, w_query, b_query, w_key, b_key, w_value, b_value,
    page_owner, page_slot,
):
    phase, rep, tp = lax.axis_index("phase"), lax.axis_index("rep"), lax.axis_index("tp")
    n_phase, n_rep = lax.axis_size("phase"), lax.axis_size("rep")
    groups = n_phase * n_rep
    group = phase * n_rep + rep
    chip, core = tp // 2, tp % 2
    bf16, f32 = jnp.bfloat16, jnp.float32

    tp_ways = lax.axis_size("tp")
    chips = tp_ways // 2
    across = lambda a, by: lax.ppermute(
        a, "tp", [(i, (i + 2 * by) % tp_ways) for i in range(tp_ways)]
    )
    partner = lambda a: lax.ppermute(a, "tp", [(i, i ^ 1) for i in range(tp_ways)])
    take = lambda a, at: lax.dynamic_index_in_dim(a, at, 0, keepdims=False)

    owner, owners = img_owner[0], page_owner[0]

    depth = w_query.shape[0]
    gain = lax.dynamic_slice_in_dim(lang_gain, group * depth, depth)[:, None]
    own = scale(gain, w_query, w_key, w_value)

    weights = lax.all_gather(own, ("phase", "rep"), axis=0, tiled=True)
    x_near = [across(prompt_rows, by) for by in (1, -1)]

    patch_count, width = patches.shape
    merge = 4
    order = window_order[0].reshape(patch_count // merge, merge).T[:, :, None]
    chunks = vis_qkv.shape[1] // VHD
    bias_pad = jnp.pad(vis_qkv_bias.reshape(chunks, VHD), ((0, 0), (0, LANE - VHD))).reshape(1, -1)
    keep, send, resid = vision_partial(
        order, patches, vis_gain, vis_qkv.T, bias_pad, vis_proj, jnp.stack([core, chip])
    )
    keep, send, resid, x_own, *x_near = after((keep, send, resid, prompt_rows, *x_near))

    x_far = across(x_own, 2)
    chip_sum = (keep.astype(f32) + partner(send).astype(f32)).astype(bf16)
    dest_iota = jnp.arange(groups, dtype=jnp.int32)
    to_images = jnp.sum(
        jnp.where(owner[None, :] == dest_iota[:, None], img_slot + 1, 0), axis=1, keepdims=True
    )
    pages = owners.shape[0]
    rows = prompt_rows.shape[0]
    page_rows = rows // pages
    page_iota = jnp.arange(pages, dtype=jnp.int32)
    first_of = lambda ids: jnp.min(
        jnp.where(ids[..., :, None] == ids[..., None, :], page_iota, pages), axis=-1
    )
    first_page = first_of(owners)
    owner_group = phase * n_rep + owners
    hit = (owner_group[None, None, :] == dest_iota[:, None, None]) & (
        (page_iota - first_page)[None, None, :] == jnp.arange(7, dtype=jnp.int32)[None, :, None]
    )
    to_pages = jnp.sum(jnp.where(hit, page_slot[0] + 1, 0), axis=2)
    routes = lax.all_to_all(
        jnp.concatenate([to_images, to_pages], axis=1), ("phase", "rep"), split_axis=0,
        concat_axis=0, tiled=True,
    )
    start = jnp.repeat(first_page, page_rows) * page_rows
    position = jnp.arange(rows, dtype=jnp.int32) - start
    half_dim = HD // 2
    inv_freq = jnp.exp(-jnp.log(1000000.0) * jnp.arange(half_dim).astype(f32) / half_dim)
    angles = position.astype(f32)[:, None] * inv_freq[None, :]
    cosine, sines = jnp.cos(angles), jnp.sin(angles)
    cosine = jnp.concatenate([cosine, cosine], axis=1)
    sines = jnp.concatenate([-sines, sines], axis=1)
    chip_sum, x_far, x_own, routes, cosine, sines = after(
        (chip_sum, x_far, x_own, routes, cosine, sines)
    )

    arrived = [across(take(chip_sum, (chip + by) % chips), by) for by in (1, -1, 2)]
    x_side = join(x_own, *x_near, x_far)
    x_other = partner(x_side)
    half = width // 2
    cols = lambda a: lax.dynamic_slice_in_dim(a, core * half, half, a.ndim - 1)
    mixed = resid.astype(f32) + cols(vis_proj_bias)
    for part in [take(chip_sum, chip)] + arrived:
        mixed = mixed + part.astype(f32)
    squares = jnp.sum(mixed * mixed, axis=-1).reshape(2, -1)
    squares = squares + partner(squares)
    factor = lax.rsqrt(squares.reshape(-1, 1) / width + EPS)
    merged = (mixed * factor * cols(merge_gain)).astype(bf16)
    requests = owner.shape[0]
    merged = merged.reshape(requests, -1, half)
    outgoing = place(owner, merged, groups)
    outgoing, x_other = after((outgoing, x_other))

    images = lax.all_to_all(outgoing, ("phase", "rep"), split_axis=0, concat_axis=0, tiled=True)
    ways = jnp.stack(
        [((chip - by) % chips) * 2 + side for side in (core, 1 - core) for by in (0, 1, -1, 2)]
    ).astype(jnp.int32)
    x, row_factor = ordered(ways, rows, (x_side, x_other))

    image_at = routes[:, 0] - 1
    page_at = lax.dynamic_slice_in_dim(routes, phase * n_rep, n_rep, 0)[:, 1 : 1 + CAP] - 1
    page_at = page_at.reshape(-1)
    image_buffer = place(image_at, images, groups).reshape(-1, half)
    dest = (owners * CAP + page_iota - first_page).astype(jnp.int32)
    weights, image_buffer, page_at, start, x, row_factor, dest = after(
        (weights, image_buffer, page_at, start[:, None], x, row_factor, dest)
    )

    kv, outgoing_pages = kv_rows(
        dest, x, weights, row_factor, jnp.concatenate([b_key, b_value])[None, :], cosine, sines,
        n_rep * CAP, page_rows,
    )
    arrived_pages = lax.all_to_all(
        outgoing_pages.reshape(n_rep, CAP, page_rows, -1), "rep", split_axis=0, concat_axis=0, tiled=True
    )
    attn_out = attend(x, weights, row_factor, b_query[None, :], cosine, sines, start, kv)
    kv_pool = place(page_at, arrived_pages.reshape(n_rep * CAP, page_rows, -1), pages)
    return (image_buffer, attn_out, kv_pool)


def solution(mesh):
    split, cut = P(("phase", "rep"), None), P(("phase", "rep"), "tp")
    return jax.shard_map(
        body,
        mesh=mesh,
        in_specs=(
            split, split, P(), P(None, "tp"), P("tp"), P("tp", None), P(), P(), split, split,
            cut, P(), cut, P("tp"), cut, P("tp"), cut, P("tp"), split, split,
        ),
        out_specs=(cut, cut, P(("phase", "rep"), None, "tp")),
        check_vma=False,
    )
```

```python
import jax
import jax.numpy as jnp
from jax import lax
from jax.experimental import pallas as pl
from jax.experimental.pallas import tpu as pltpu
from jax.sharding import PartitionSpec as P

VD = 1280
VHD = 80
LANE = 128
HD = 128
EPS = 1e-06
CAP = 5
AHEAD = 3
WINDOW = 384
VMEM_LIMIT = 58 * 1024 * 1024


def resident():
    return pl.BlockSpec(memory_space=pltpu.VMEM)


def whole(shape):
    return pl.BlockSpec(shape, lambda *_: (0,) * len(shape))


def params(limit=VMEM_LIMIT):
    return pltpu.CompilerParams(vmem_limit_bytes=limit)


def cheap():
    return pl.CostEstimate(flops=1_000_000, bytes_accessed=1000, transcendentals=0)


def vision_kernel(own_ref, order_ref, patches_ref, gain_ref, w_ref, bias_ref, proj_ref, *refs):
    keep_ref, send_ref, resid_ref, w_pad, proj_pad, held, apart = refs[-7:]
    parts, span, width = held.shape
    total = parts * span
    chunks = w_ref.shape[0] // VHD
    core, chip = own_ref[0], own_ref[1]

    @pl.when(pl.program_id(0) == 0)
    def _():
        w_pad[...] = jnp.zeros_like(w_pad)
        proj_pad[...] = jnp.zeros_like(proj_pad)
        for pad, ref in ((w_pad, w_ref), (proj_pad, proj_ref)):
            for at in range(ref.shape[0] // VHD):
                pad[at * LANE : at * LANE + VHD] = ref[at * VHD : (at + 1) * VHD]
        window_q = (lax.broadcasted_iota(jnp.int32, (total, total), 0) & (span - 1)) >> 4
        window_k = (lax.broadcasted_iota(jnp.int32, (total, total), 1) & (span - 1)) >> 4
        apart[...] = jnp.where(window_q == window_k, 0.0, -1e30)

    places = patches_ref.shape[0]
    wanted = order_ref[...].reshape(total, 1)
    onehot = jnp.where(
        wanted == lax.broadcasted_iota(jnp.int32, (total, places), 1), 1.0, 0.0
    ).astype(jnp.bfloat16)
    rows = jnp.dot(onehot, patches_ref[...], preferred_element_type=jnp.float32)
    held[...] = rows.astype(jnp.bfloat16).reshape(parts, span, width)
    half = width // 2
    mine = pl.multiple_of(core * half, LANE)
    other = pl.multiple_of((1 - core) * half, LANE)
    resid_ref[...] = held[chip, :, pl.ds(mine, half)]
    factor = lax.rsqrt(jnp.mean(rows * rows, axis=-1, keepdims=True) + EPS)
    normed = (rows * factor * gain_ref[...][None, :]).astype(jnp.bfloat16)
    projected = lax.dot_general(
        normed, w_pad[...], (((1,), (1,)), ((), ())), preferred_element_type=jnp.float32
    )
    projected = (projected + bias_ref[...]).astype(jnp.bfloat16)
    heads = []
    for head in range(chunks // 3):
        at = head * 3 * LANE
        query = projected[:, at : at + LANE]
        keyed = projected[:, at + LANE : at + 2 * LANE]
        valued = projected[:, at + 2 * LANE : at + 3 * LANE]
        scores = lax.dot_general(
            query, keyed, (((1,), (1,)), ((), ())), preferred_element_type=jnp.float32
        )
        scores = scores * (VHD ** (-0.5)) + apart[...]
        raised = jnp.exp(scores - jnp.max(scores, axis=-1, keepdims=True))
        scale_back = 1.0 / jnp.sum(raised, axis=-1, keepdims=True)
        weights = raised.astype(jnp.bfloat16)
        mixed = jnp.dot(weights, valued, preferred_element_type=jnp.float32) * scale_back
        heads.append(mixed.astype(jnp.bfloat16))
    mixed = jnp.concatenate(heads, axis=1)
    for out_ref, at in ((keep_ref, mine), (send_ref, other)):
        part = jnp.dot(mixed, proj_pad[:, pl.ds(at, half)], preferred_element_type=jnp.float32)
        out_ref[...] = part.astype(jnp.bfloat16).reshape(parts, span, half)


def vision_partial(order, patches, gain, w, bias_pad, proj, own):
    parts, span, _ = order.shape
    width = patches.shape[1]
    step = 64
    half = width // 2
    chunks = w.shape[0] // VHD
    spec = pl.BlockSpec((parts, step, half), lambda i, _: (0, i, 0))
    out = jax.ShapeDtypeStruct((parts, span, half), jnp.bfloat16)
    return pl.pallas_call(
        vision_kernel,
        grid_spec=pltpu.PrefetchScalarGridSpec(
            num_scalar_prefetch=1,
            grid=(span // step,),
            in_specs=[
                pl.BlockSpec((parts, step, 1), lambda i, _: (0, i, 0)),
                whole(patches.shape),
                whole(gain.shape),
                whole(w.shape),
                whole(bias_pad.shape),
                whole(proj.shape),
            ],
            out_specs=[spec, spec, pl.BlockSpec((step, half), lambda i, _: (i, 0))],
            scratch_shapes=[
                pltpu.VMEM((chunks * LANE, width), jnp.bfloat16),
                pltpu.VMEM((chunks // 3 * LANE, width), jnp.bfloat16),
                pltpu.VMEM((parts, step, width), jnp.bfloat16),
                pltpu.VMEM((parts * step, parts * step), jnp.float32),
            ],
        ),
        out_shape=[out, out, jax.ShapeDtypeStruct((span, half), jnp.bfloat16)],
        compiler_params=params(),
        cost_estimate=pl.CostEstimate(
            flops=14_000_000_000, bytes_accessed=6_000_000, transcendentals=0
        ),
    )(own, order, patches, gain, w, bias_pad, proj)


def join_kernel(*refs):
    out_ref = refs[-1]
    at = 0
    for ref in refs[:-1]:
        out_ref[at : at + ref.shape[0]] = ref[...]
        at += ref.shape[0]


def join(*parts):
    shape = (sum(part.shape[0] for part in parts),) + parts[0].shape[1:]
    return pl.pallas_call(
        join_kernel,
        grid=(1,),
        in_specs=[whole(part.shape) for part in parts],
        out_specs=whole(shape),
        out_shape=jax.ShapeDtypeStruct(shape, parts[0].dtype),
        compiler_params=params(),
    )(*parts)


def scale_kernel(gain_ref, query_ref, key_ref, value_ref, out_ref):
    gain = gain_ref[...]
    at = 0
    for ref in (key_ref, value_ref, query_ref):
        width = ref.shape[1]
        scaled = ref[...].astype(jnp.float32) * gain
        out_ref[:, at : at + width] = scaled.astype(jnp.bfloat16)
        at += width


def scale(gain, w_query, w_key, w_value):
    parts = (gain, w_query, w_key, w_value)
    shape = (w_query.shape[0], sum(part.shape[1] for part in parts[1:]))
    return pl.pallas_call(
        scale_kernel,
        grid=(1,),
        in_specs=[whole(part.shape) for part in parts],
        out_specs=whole(shape),
        out_shape=jax.ShapeDtypeStruct(shape, jnp.bfloat16),
        compiler_params=params(),
    )(*parts)


def place_kernel(at_ref, items_ref, out_ref):
    out_ref[...] = jnp.zeros_like(out_ref)
    for index in range(items_ref.shape[0]):
        at = at_ref[index]

        @pl.when(at >= 0)
        def _():
            out_ref[pl.ds(at, 1)] = items_ref[index : index + 1]


def place(at, items, slots):
    shape = (slots,) + items.shape[1:]
    return pl.pallas_call(
        place_kernel,
        grid_spec=pltpu.PrefetchScalarGridSpec(
            num_scalar_prefetch=1,
            grid=(1,),
            in_specs=[whole(items.shape)],
            out_specs=whole(shape),
        ),
        out_shape=jax.ShapeDtypeStruct(shape, items.dtype),
        compiler_params=params(),
    )(at, items)


def pool_kernel(at_ref, items_ref, out_ref, sems):
    def copy(index):
        return pltpu.make_async_copy(
            items_ref.at[index], out_ref.at[at_ref[index]], sems.at[index]
        )

    for index in range(items_ref.shape[0]):

        @pl.when(at_ref[index] >= 0)
        def _():
            copy(index).start()

    for index in range(items_ref.shape[0]):

        @pl.when(at_ref[index] >= 0)
        def _():
            copy(index).wait()


def pool(at, items, slots):
    return pl.pallas_call(
        pool_kernel,
        in_specs=[pl.BlockSpec(memory_space=pltpu.SMEM), anywhere()],
        out_specs=anywhere(),
        out_shape=jax.ShapeDtypeStruct((slots,) + items.shape[1:], items.dtype),
        scratch_shapes=[pltpu.SemaphoreType.DMA((items.shape[0],))],
        compiler_params=params(),
    )(at, items)


def rotary(values, cosine, sines):
    return values * cosine + pltpu.roll(values, HD // 2, 1) * sines


def anywhere():
    return pl.BlockSpec(memory_space=pl.ANY)


def order_kernel(ways_ref, *refs):
    x_refs, (out_ref, factor_ref, held, sems) = refs[:-4], refs[-4:]
    parts, rows, part = held.shape
    each = parts // len(x_refs)
    loads, stores = [], []
    for index in range(parts):
        at = index % each * rows
        source = x_refs[index // each].at[at : at + rows]
        loads.append(pltpu.make_async_copy(source, held.at[index], sems.at[index]))
        stores.append(
            pltpu.make_async_copy(
                held.at[index], out_ref.at[ways_ref[index]], sems.at[parts + index]
            )
        )
    for load in loads[:AHEAD]:
        load.start()
    squares = jnp.zeros((rows, LANE), jnp.float32)
    for index in range(parts):
        loads[index].wait()
        stores[index].start()
        for load in loads[index + AHEAD : index + AHEAD + 1]:
            load.start()
        for at in range(0, part, LANE):
            wide = held[index, :, at : at + LANE].astype(jnp.float32)
            squares += wide * wide
    squares = jnp.sum(squares, axis=-1, keepdims=True)
    factor_ref[...] = lax.rsqrt(squares / (parts * part) + EPS)
    for store in stores:
        store.wait()


def ordered(ways, rows, xs):
    parts, part = ways.shape[0], xs[0].shape[1]
    return pl.pallas_call(
        order_kernel,
        in_specs=[pl.BlockSpec(memory_space=pltpu.SMEM)] + [anywhere()] * len(xs),
        out_specs=[anywhere(), resident()],
        out_shape=[
            jax.ShapeDtypeStruct((parts, rows, part), jnp.bfloat16),
            jax.ShapeDtypeStruct((rows, 1), jnp.float32),
        ],
        scratch_shapes=[
            pltpu.VMEM((parts, rows, part), jnp.bfloat16),
            pltpu.SemaphoreType.DMA((2 * parts,)),
        ],
        compiler_params=params(),
        cost_estimate=cheap(),
    )(ways, *xs)


def kv_kernel(dest_ref, x_ref, w_ref, *refs):
    factor_ref, bias_ref, cos_ref, sin_ref, out_ref, pages_ref = refs[:6]
    x_held, held, sems = refs[6:]
    parts, rows, part = x_held.shape
    width = held.shape[2]
    loads = []
    for i in range(parts):
        rows_of = w_ref.at[i * part : (i + 1) * part, :width]
        loads.append(pltpu.make_async_copy(x_ref.at[i], x_held.at[i], sems.at[2 * i]))
        loads.append(pltpu.make_async_copy(rows_of, held.at[i], sems.at[2 * i + 1]))
    for copy in loads[: 2 * AHEAD]:
        copy.start()
    pages_ref[...] = jnp.zeros_like(pages_ref)
    total = jnp.zeros(out_ref.shape, jnp.float32)
    for index in range(parts):
        loads[2 * index].wait()
        loads[2 * index + 1].wait()
        for copy in loads[2 * (index + AHEAD) : 2 * (index + AHEAD + 1)]:
            copy.start()
        total += jnp.dot(x_held[index], held[index], preferred_element_type=jnp.float32)
    total = total * factor_ref[...] + bias_ref[...]
    out_ref[:, :HD] = rotary(total[:, :HD], cos_ref[...], sin_ref[...]).astype(jnp.bfloat16)
    out_ref[:, HD:] = total[:, HD:].astype(jnp.bfloat16)
    page_rows = pages_ref.shape[1]
    for page in range(rows // page_rows):
        pages_ref[pl.ds(dest_ref[page], 1)] = out_ref[
            page * page_rows : (page + 1) * page_rows, :
        ][None]


def kv_rows(dest, x, w, factor, bias, cosine, sines, slots, page_rows):
    parts, rows, part = x.shape
    width = bias.shape[1]
    small = (factor, bias, cosine, sines)
    shapes = [(rows, width), (slots, page_rows, width)]
    return pl.pallas_call(
        kv_kernel,
        in_specs=[pl.BlockSpec(memory_space=pltpu.SMEM)]
        + [anywhere()] * 2
        + [resident()] * len(small),
        out_specs=[resident()] * 2,
        out_shape=[jax.ShapeDtypeStruct(shape, jnp.bfloat16) for shape in shapes],
        scratch_shapes=[
            pltpu.VMEM(x.shape, jnp.bfloat16),
            pltpu.VMEM((parts, part, width), jnp.bfloat16),
            pltpu.SemaphoreType.DMA((2 * parts,)),
        ],
        compiler_params=params(),
        cost_estimate=pl.CostEstimate(
            flops=7_000_000_000, bytes_accessed=13_000_000, transcendentals=0
        ),
    )(dest, x, w, *small)


def attend_kernel(x_ref, w_ref, *refs):
    factor_ref, bias_ref, cos_ref, sin_ref, start_ref, kv_ref, out_ref = refs[:7]
    x_held, held, sems = refs[7:]
    parts, rows, part = x_held.shape
    skip = w_ref.shape[1] - held.shape[2]
    loads = []
    for i in range(parts):
        rows_of = w_ref.at[i * part : (i + 1) * part, skip:]
        loads.append(pltpu.make_async_copy(x_ref.at[i], x_held.at[i], sems.at[2 * i]))
        loads.append(pltpu.make_async_copy(rows_of, held.at[i], sems.at[2 * i + 1]))
    for copy in loads[: 2 * AHEAD]:
        copy.start()
    total = jnp.zeros(out_ref.shape, jnp.float32)
    for index in range(parts):
        loads[2 * index].wait()
        loads[2 * index + 1].wait()
        for copy in loads[2 * (index + AHEAD) : 2 * (index + AHEAD + 1)]:
            copy.start()
        total += jnp.dot(x_held[index], held[index], preferred_element_type=jnp.float32)
    total = total * factor_ref[...] + bias_ref[...]
    step = 256
    for first in range(0, rows, step):
        span = slice(first, first + step)
        begin = max(first + step - WINDOW, 0)
        end = first + step
        keyed = kv_ref[begin:end, :HD]
        valued = kv_ref[begin:end, HD:]
        key_at = begin + lax.broadcasted_iota(jnp.int32, (step, end - begin), 1)
        row_at = first + lax.broadcasted_iota(jnp.int32, (step, end - begin), 0)
        allowed = (key_at <= row_at) & (key_at >= start_ref[span, :])
        cosine, sines = cos_ref[span, :], sin_ref[span, :]
        for at in range(0, total.shape[1], HD):
            query = rotary(total[span, at : at + HD], cosine, sines).astype(jnp.bfloat16)
            scores = lax.dot_general(
                query, keyed, (((1,), (1,)), ((), ())), preferred_element_type=jnp.float32
            ) * (HD ** (-0.5))
            scores = jnp.where(allowed, scores, -1e30)
            raised = jnp.exp(scores - jnp.max(scores, axis=-1, keepdims=True))
            scale_back = 1.0 / jnp.sum(raised, axis=-1, keepdims=True)
            weights = raised.astype(jnp.bfloat16)
            mixed = jnp.dot(weights, valued, preferred_element_type=jnp.float32) * scale_back
            out_ref[span, at : at + HD] = mixed.astype(jnp.bfloat16)


def attend(x, w, factor, bias, cosine, sines, start, kv):
    parts, rows, part = x.shape
    width = bias.shape[1]
    small = (factor, bias, cosine, sines, start, kv)
    return pl.pallas_call(
        attend_kernel,
        in_specs=[anywhere()] * 2 + [resident()] * len(small),
        out_specs=resident(),
        out_shape=jax.ShapeDtypeStruct((rows, width), jnp.bfloat16),
        scratch_shapes=[
            pltpu.VMEM(x.shape, jnp.bfloat16),
            pltpu.VMEM((parts, part, width), jnp.bfloat16),
            pltpu.SemaphoreType.DMA((2 * parts,)),
        ],
        compiler_params=params(),
        cost_estimate=pl.CostEstimate(
            flops=14_000_000_000, bytes_accessed=17_000_000, transcendentals=0
        ),
    )(x, w, *small)


def after(values, *others):
    return lax.optimization_barrier((tuple(values),) + others)[0]


def body(
    patches, window_order, vis_gain, vis_qkv, vis_qkv_bias, vis_proj, vis_proj_bias, merge_gain,
    img_owner, img_slot, prompt_rows, lang_gain, w_query, b_query, w_key, b_key, w_value, b_value,
    page_owner, page_slot,
):
    phase, rep, tp = lax.axis_index("phase"), lax.axis_index("rep"), lax.axis_index("tp")
    n_phase, n_rep = lax.axis_size("phase"), lax.axis_size("rep")
    groups = n_phase * n_rep
    group = phase * n_rep + rep
    chip, core = tp // 2, tp % 2
    bf16, f32 = jnp.bfloat16, jnp.float32

    tp_ways = lax.axis_size("tp")
    chips = tp_ways // 2
    across = lambda a, by: lax.ppermute(
        a, "tp", [(i, (i + 2 * by) % tp_ways) for i in range(tp_ways)]
    )
    partner = lambda a: lax.ppermute(a, "tp", [(i, i ^ 1) for i in range(tp_ways)])
    take = lambda a, at: lax.dynamic_index_in_dim(a, at, 0, keepdims=False)

    owner, owners = img_owner[0], page_owner[0]

    depth = w_query.shape[0]
    gain = lax.dynamic_slice_in_dim(lang_gain, group * depth, depth)[:, None]
    own = scale(gain, w_query, w_key, w_value)

    weights = lax.all_gather(own, ("phase", "rep"), axis=0, tiled=True)
    x_near = [across(prompt_rows, by) for by in (1, -1)]

    patch_count, width = patches.shape
    merge = 4
    order = window_order[0].reshape(patch_count // merge, merge).T[:, :, None]
    chunks = vis_qkv.shape[1] // VHD
    bias_pad = jnp.pad(vis_qkv_bias.reshape(chunks, VHD), ((0, 0), (0, LANE - VHD))).reshape(1, -1)
    keep, send, resid = vision_partial(
        order, patches, vis_gain, vis_qkv.T, bias_pad, vis_proj, jnp.stack([core, chip])
    )
    keep, send, resid, x_own, *x_near = after((keep, send, resid, prompt_rows, *x_near))

    x_far = across(x_own, 2)
    chip_sum = (keep.astype(f32) + partner(send).astype(f32)).astype(bf16)
    dest_iota = jnp.arange(groups, dtype=jnp.int32)
    to_images = jnp.sum(
        jnp.where(owner[None, :] == dest_iota[:, None], img_slot + 1, 0), axis=1, keepdims=True
    )
    pages = owners.shape[0]
    rows = prompt_rows.shape[0]
    page_rows = rows // pages
    page_iota = jnp.arange(pages, dtype=jnp.int32)
    first_of = lambda ids: jnp.min(
        jnp.where(ids[..., :, None] == ids[..., None, :], page_iota, pages), axis=-1
    )
    first_page = first_of(owners)
    owner_group = phase * n_rep + owners
    hit = (owner_group[None, None, :] == dest_iota[:, None, None]) & (
        (page_iota - first_page)[None, None, :] == jnp.arange(7, dtype=jnp.int32)[None, :, None]
    )
    to_pages = jnp.sum(jnp.where(hit, page_slot[0] + 1, 0), axis=2)
    routes = lax.all_to_all(
        jnp.concatenate([to_images, to_pages], axis=1), ("phase", "rep"), split_axis=0,
        concat_axis=0, tiled=True,
    )
    start = jnp.repeat(first_page, page_rows) * page_rows
    position = jnp.arange(rows, dtype=jnp.int32) - start
    half_dim = HD // 2
    inv_freq = jnp.exp(-jnp.log(1000000.0) * jnp.arange(half_dim).astype(f32) / half_dim)
    angles = position.astype(f32)[:, None] * inv_freq[None, :]
    cosine, sines = jnp.cos(angles), jnp.sin(angles)
    cosine = jnp.concatenate([cosine, cosine], axis=1)
    sines = jnp.concatenate([-sines, sines], axis=1)
    chip_sum, x_far, x_own, routes, cosine, sines = after(
        (chip_sum, x_far, x_own, routes, cosine, sines)
    )

    x_side = join(x_own, *x_near, x_far)
    ways = jnp.stack(
        [((chip - by) % chips) * 2 + side for side in (core, 1 - core) for by in (0, 1, -1, 2)]
    ).astype(jnp.int32)
    x, row_factor = ordered(ways, rows, (x_side, partner(x_side)))
    chip_sum, x, row_factor = after((chip_sum, x, row_factor))

    arrived = [across(take(chip_sum, (chip + by) % chips), by) for by in (1, -1, 2)]
    half = width // 2
    cols = lambda a: lax.dynamic_slice_in_dim(a, core * half, half, a.ndim - 1)
    mixed = resid.astype(f32) + cols(vis_proj_bias)
    for part in [take(chip_sum, chip)] + arrived:
        mixed = mixed + part.astype(f32)
    squares = jnp.sum(mixed * mixed, axis=-1).reshape(2, -1)
    squares = squares + partner(squares)
    factor = lax.rsqrt(squares.reshape(-1, 1) / width + EPS)
    merged = (mixed * factor * cols(merge_gain)).astype(bf16)
    requests = owner.shape[0]
    merged = merged.reshape(requests, -1, half)
    outgoing = place(owner, merged, groups)
    images = lax.all_to_all(outgoing, ("phase", "rep"), split_axis=0, concat_axis=0, tiled=True)

    image_at = routes[:, 0] - 1
    page_at = lax.dynamic_slice_in_dim(routes, phase * n_rep, n_rep, 0)[:, 1 : 1 + CAP] - 1
    page_at = page_at.reshape(-1)
    dest = (owners * CAP + page_iota - first_page).astype(jnp.int32)
    weights, outgoing, page_at, start, dest = after(
        (weights, outgoing, page_at, start[:, None], dest)
    )

    kv, outgoing_pages = kv_rows(
        dest, x, weights, row_factor, jnp.concatenate([b_key, b_value])[None, :], cosine, sines,
        n_rep * CAP, page_rows,
    )
    arrived_pages = lax.all_to_all(
        outgoing_pages.reshape(n_rep, CAP, page_rows, -1), "rep", split_axis=0, concat_axis=0, tiled=True
    )
    (images,) = after((images,), kv)
    image_buffer = place(image_at, images, groups).reshape(-1, half)
    attn_out = attend(x, weights, row_factor, b_query[None, :], cosine, sines, start, kv)
    kv_pool = pool(page_at, arrived_pages.reshape(n_rep * CAP, page_rows, -1), pages)
    return (image_buffer, attn_out, kv_pool)


def solution(mesh):
    split, cut = P(("phase", "rep"), None), P(("phase", "rep"), "tp")
    return jax.shard_map(
        body,
        mesh=mesh,
        in_specs=(
            split, split, P(), P(None, "tp"), P("tp"), P("tp", None), P(), P(), split, split,
            cut, P(), cut, P("tp"), cut, P("tp"), cut, P("tp"), split, split,
        ),
        out_specs=(cut, cut, P(("phase", "rep"), None, "tp")),
        check_vma=False,
    )
```

```python
import jax
import jax.numpy as jnp
from jax import lax
from jax.experimental import pallas as pl
from jax.experimental.pallas import tpu as pltpu
from jax.sharding import PartitionSpec as P

VD = 1280
VHD = 80
LANE = 128
HD = 128
EPS = 1e-06
CAP = 5
AHEAD = 3
WINDOW = 384
VMEM_LIMIT = 58 * 1024 * 1024


def resident():
    return pl.BlockSpec(memory_space=pltpu.VMEM)


def whole(shape):
    return pl.BlockSpec(shape, lambda *_: (0,) * len(shape))


def params(limit=VMEM_LIMIT):
    return pltpu.CompilerParams(vmem_limit_bytes=limit)


def cheap():
    return pl.CostEstimate(flops=1_000_000, bytes_accessed=1000, transcendentals=0)


def vision_kernel(own_ref, order_ref, patches_ref, gain_ref, w_ref, bias_ref, proj_ref, *refs):
    keep_ref, send_ref, resid_ref, w_pad, proj_pad, held, apart = refs[-7:]
    parts, span, width = held.shape
    total = parts * span
    chunks = w_ref.shape[0] // VHD
    core, chip = own_ref[0], own_ref[1]

    @pl.when(pl.program_id(0) == 0)
    def _():
        w_pad[...] = jnp.zeros_like(w_pad)
        proj_pad[...] = jnp.zeros_like(proj_pad)
        for pad, ref in ((w_pad, w_ref), (proj_pad, proj_ref)):
            for at in range(ref.shape[0] // VHD):
                pad[at * LANE : at * LANE + VHD] = ref[at * VHD : (at + 1) * VHD]
        window_q = (lax.broadcasted_iota(jnp.int32, (total, total), 0) & (span - 1)) >> 4
        window_k = (lax.broadcasted_iota(jnp.int32, (total, total), 1) & (span - 1)) >> 4
        apart[...] = jnp.where(window_q == window_k, 0.0, -1e30)

    places = patches_ref.shape[0]
    wanted = order_ref[...].reshape(total, 1)
    onehot = jnp.where(
        wanted == lax.broadcasted_iota(jnp.int32, (total, places), 1), 1.0, 0.0
    ).astype(jnp.bfloat16)
    rows = jnp.dot(onehot, patches_ref[...], preferred_element_type=jnp.float32)
    held[...] = rows.astype(jnp.bfloat16).reshape(parts, span, width)
    half = width // 2
    mine = pl.multiple_of(core * half, LANE)
    other = pl.multiple_of((1 - core) * half, LANE)
    resid_ref[...] = held[chip, :, pl.ds(mine, half)]
    factor = lax.rsqrt(jnp.mean(rows * rows, axis=-1, keepdims=True) + EPS)
    normed = (rows * factor * gain_ref[...][None, :]).astype(jnp.bfloat16)
    projected = lax.dot_general(
        normed, w_pad[...], (((1,), (1,)), ((), ())), preferred_element_type=jnp.float32
    )
    projected = (projected + bias_ref[...]).astype(jnp.bfloat16)
    heads = []
    for head in range(chunks // 3):
        at = head * 3 * LANE
        query = projected[:, at : at + LANE]
        keyed = projected[:, at + LANE : at + 2 * LANE]
        valued = projected[:, at + 2 * LANE : at + 3 * LANE]
        scores = lax.dot_general(
            query, keyed, (((1,), (1,)), ((), ())), preferred_element_type=jnp.float32
        )
        scores = scores * (VHD ** (-0.5)) + apart[...]
        raised = jnp.exp(scores - jnp.max(scores, axis=-1, keepdims=True))
        scale_back = 1.0 / jnp.sum(raised, axis=-1, keepdims=True)
        weights = raised.astype(jnp.bfloat16)
        mixed = jnp.dot(weights, valued, preferred_element_type=jnp.float32) * scale_back
        heads.append(mixed.astype(jnp.bfloat16))
    mixed = jnp.concatenate(heads, axis=1)
    for out_ref, at in ((keep_ref, mine), (send_ref, other)):
        part = jnp.dot(mixed, proj_pad[:, pl.ds(at, half)], preferred_element_type=jnp.float32)
        out_ref[...] = part.astype(jnp.bfloat16).reshape(parts, span, half)


def vision_partial(order, patches, gain, w, bias_pad, proj, own):
    parts, span, _ = order.shape
    width = patches.shape[1]
    step = 64
    half = width // 2
    chunks = w.shape[0] // VHD
    spec = pl.BlockSpec((parts, step, half), lambda i, _: (0, i, 0))
    out = jax.ShapeDtypeStruct((parts, span, half), jnp.bfloat16)
    return pl.pallas_call(
        vision_kernel,
        grid_spec=pltpu.PrefetchScalarGridSpec(
            num_scalar_prefetch=1,
            grid=(span // step,),
            in_specs=[
                pl.BlockSpec((parts, step, 1), lambda i, _: (0, i, 0)),
                whole(patches.shape),
                whole(gain.shape),
                whole(w.shape),
                whole(bias_pad.shape),
                whole(proj.shape),
            ],
            out_specs=[spec, spec, pl.BlockSpec((step, half), lambda i, _: (i, 0))],
            scratch_shapes=[
                pltpu.VMEM((chunks * LANE, width), jnp.bfloat16),
                pltpu.VMEM((chunks // 3 * LANE, width), jnp.bfloat16),
                pltpu.VMEM((parts, step, width), jnp.bfloat16),
                pltpu.VMEM((parts * step, parts * step), jnp.float32),
            ],
        ),
        out_shape=[out, out, jax.ShapeDtypeStruct((span, half), jnp.bfloat16)],
        compiler_params=params(),
        cost_estimate=pl.CostEstimate(
            flops=14_000_000_000, bytes_accessed=6_000_000, transcendentals=0
        ),
    )(own, order, patches, gain, w, bias_pad, proj)


def join_kernel(*refs):
    out_ref = refs[-1]
    at = 0
    for ref in refs[:-1]:
        out_ref[at : at + ref.shape[0]] = ref[...]
        at += ref.shape[0]


def join(*parts):
    shape = (sum(part.shape[0] for part in parts),) + parts[0].shape[1:]
    return pl.pallas_call(
        join_kernel,
        grid=(1,),
        in_specs=[whole(part.shape) for part in parts],
        out_specs=whole(shape),
        out_shape=jax.ShapeDtypeStruct(shape, parts[0].dtype),
        compiler_params=params(),
    )(*parts)


def scale_kernel(gain_ref, query_ref, key_ref, value_ref, out_ref):
    gain = gain_ref[...]
    at = 0
    for ref in (key_ref, value_ref, query_ref):
        width = ref.shape[1]
        scaled = ref[...].astype(jnp.float32) * gain
        out_ref[:, at : at + width] = scaled.astype(jnp.bfloat16)
        at += width


def scale(gain, w_query, w_key, w_value):
    parts = (gain, w_query, w_key, w_value)
    shape = (w_query.shape[0], sum(part.shape[1] for part in parts[1:]))
    return pl.pallas_call(
        scale_kernel,
        grid=(1,),
        in_specs=[whole(part.shape) for part in parts],
        out_specs=whole(shape),
        out_shape=jax.ShapeDtypeStruct(shape, jnp.bfloat16),
        compiler_params=params(),
    )(*parts)


def place_kernel(at_ref, items_ref, out_ref):
    out_ref[...] = jnp.zeros_like(out_ref)
    for index in range(items_ref.shape[0]):
        at = at_ref[index]

        @pl.when(at >= 0)
        def _():
            out_ref[pl.ds(at, 1)] = items_ref[index : index + 1]


def place(at, items, slots):
    shape = (slots,) + items.shape[1:]
    return pl.pallas_call(
        place_kernel,
        grid_spec=pltpu.PrefetchScalarGridSpec(
            num_scalar_prefetch=1,
            grid=(1,),
            in_specs=[whole(items.shape)],
            out_specs=whole(shape),
        ),
        out_shape=jax.ShapeDtypeStruct(shape, items.dtype),
        compiler_params=params(),
    )(at, items)


def rotary(values, cosine, sines):
    return values * cosine + pltpu.roll(values, HD // 2, 1) * sines


def anywhere():
    return pl.BlockSpec(memory_space=pl.ANY)


def order_kernel(ways_ref, *refs):
    x_refs, (out_ref, factor_ref, held, sems) = refs[:-4], refs[-4:]
    parts, rows, part = held.shape
    each = parts // len(x_refs)
    loads, stores = [], []
    for index in range(parts):
        at = index % each * rows
        source = x_refs[index // each].at[at : at + rows]
        loads.append(pltpu.make_async_copy(source, held.at[index], sems.at[index]))
        stores.append(
            pltpu.make_async_copy(
                held.at[index], out_ref.at[ways_ref[index]], sems.at[parts + index]
            )
        )
    for load in loads[:AHEAD]:
        load.start()
    squares = jnp.zeros((rows, LANE), jnp.float32)
    for index in range(parts):
        loads[index].wait()
        stores[index].start()
        for load in loads[index + AHEAD : index + AHEAD + 1]:
            load.start()
        for at in range(0, part, LANE):
            wide = held[index, :, at : at + LANE].astype(jnp.float32)
            squares += wide * wide
    squares = jnp.sum(squares, axis=-1, keepdims=True)
    factor_ref[...] = lax.rsqrt(squares / (parts * part) + EPS)
    for store in stores:
        store.wait()


def ordered(ways, rows, xs):
    parts, part = ways.shape[0], xs[0].shape[1]
    return pl.pallas_call(
        order_kernel,
        in_specs=[pl.BlockSpec(memory_space=pltpu.SMEM)] + [anywhere()] * len(xs),
        out_specs=[anywhere(), resident()],
        out_shape=[
            jax.ShapeDtypeStruct((parts, rows, part), jnp.bfloat16),
            jax.ShapeDtypeStruct((rows, 1), jnp.float32),
        ],
        scratch_shapes=[
            pltpu.VMEM((parts, rows, part), jnp.bfloat16),
            pltpu.SemaphoreType.DMA((2 * parts,)),
        ],
        compiler_params=params(),
        cost_estimate=cheap(),
    )(ways, *xs)


def kv_kernel(dest_ref, x_ref, w_ref, *refs):
    factor_ref, bias_ref, cos_ref, sin_ref, out_ref, pages_ref = refs[:6]
    x_held, held, sems = refs[6:]
    parts, rows, part = x_held.shape
    width = held.shape[2]
    loads = []
    for i in range(parts):
        rows_of = w_ref.at[i * part : (i + 1) * part, :width]
        loads.append(pltpu.make_async_copy(x_ref.at[i], x_held.at[i], sems.at[2 * i]))
        loads.append(pltpu.make_async_copy(rows_of, held.at[i], sems.at[2 * i + 1]))
    for copy in loads[: 2 * AHEAD]:
        copy.start()
    pages_ref[...] = jnp.zeros_like(pages_ref)
    total = jnp.zeros(out_ref.shape, jnp.float32)
    for index in range(parts):
        loads[2 * index].wait()
        loads[2 * index + 1].wait()
        for copy in loads[2 * (index + AHEAD) : 2 * (index + AHEAD + 1)]:
            copy.start()
        total += jnp.dot(x_held[index], held[index], preferred_element_type=jnp.float32)
    total = total * factor_ref[...] + bias_ref[...]
    out_ref[:, :HD] = rotary(total[:, :HD], cos_ref[...], sin_ref[...]).astype(jnp.bfloat16)
    out_ref[:, HD:] = total[:, HD:].astype(jnp.bfloat16)
    page_rows = pages_ref.shape[1]
    for page in range(rows // page_rows):
        pages_ref[pl.ds(dest_ref[page], 1)] = out_ref[
            page * page_rows : (page + 1) * page_rows, :
        ][None]


def kv_rows(dest, x, w, factor, bias, cosine, sines, slots, page_rows):
    parts, rows, part = x.shape
    width = bias.shape[1]
    small = (factor, bias, cosine, sines)
    shapes = [(rows, width), (slots, page_rows, width)]
    return pl.pallas_call(
        kv_kernel,
        in_specs=[pl.BlockSpec(memory_space=pltpu.SMEM)]
        + [anywhere()] * 2
        + [resident()] * len(small),
        out_specs=[resident()] * 2,
        out_shape=[jax.ShapeDtypeStruct(shape, jnp.bfloat16) for shape in shapes],
        scratch_shapes=[
            pltpu.VMEM(x.shape, jnp.bfloat16),
            pltpu.VMEM((parts, part, width), jnp.bfloat16),
            pltpu.SemaphoreType.DMA((2 * parts,)),
        ],
        compiler_params=params(),
        cost_estimate=pl.CostEstimate(
            flops=7_000_000_000, bytes_accessed=13_000_000, transcendentals=0
        ),
    )(dest, x, w, *small)


def attend_kernel(x_ref, w_ref, *refs):
    factor_ref, bias_ref, cos_ref, sin_ref, start_ref, kv_ref, out_ref = refs[:7]
    x_held, held, sems = refs[7:]
    parts, rows, part = x_held.shape
    skip = w_ref.shape[1] - held.shape[2]
    loads = []
    for i in range(parts):
        rows_of = w_ref.at[i * part : (i + 1) * part, skip:]
        loads.append(pltpu.make_async_copy(x_ref.at[i], x_held.at[i], sems.at[2 * i]))
        loads.append(pltpu.make_async_copy(rows_of, held.at[i], sems.at[2 * i + 1]))
    for copy in loads[: 2 * AHEAD]:
        copy.start()
    total = jnp.zeros(out_ref.shape, jnp.float32)
    for index in range(parts):
        loads[2 * index].wait()
        loads[2 * index + 1].wait()
        for copy in loads[2 * (index + AHEAD) : 2 * (index + AHEAD + 1)]:
            copy.start()
        total += jnp.dot(x_held[index], held[index], preferred_element_type=jnp.float32)
    total = total * factor_ref[...] + bias_ref[...]
    step = 256
    for first in range(0, rows, step):
        span = slice(first, first + step)
        begin = max(first + step - WINDOW, 0)
        end = first + step
        keyed = kv_ref[begin:end, :HD]
        valued = kv_ref[begin:end, HD:]
        key_at = begin + lax.broadcasted_iota(jnp.int32, (step, end - begin), 1)
        row_at = first + lax.broadcasted_iota(jnp.int32, (step, end - begin), 0)
        allowed = (key_at <= row_at) & (key_at >= start_ref[span, :])
        cosine, sines = cos_ref[span, :], sin_ref[span, :]
        for at in range(0, total.shape[1], HD):
            query = rotary(total[span, at : at + HD], cosine, sines).astype(jnp.bfloat16)
            scores = lax.dot_general(
                query, keyed, (((1,), (1,)), ((), ())), preferred_element_type=jnp.float32
            ) * (HD ** (-0.5))
            scores = jnp.where(allowed, scores, -1e30)
            raised = jnp.exp(scores - jnp.max(scores, axis=-1, keepdims=True))
            scale_back = 1.0 / jnp.sum(raised, axis=-1, keepdims=True)
            weights = raised.astype(jnp.bfloat16)
            mixed = jnp.dot(weights, valued, preferred_element_type=jnp.float32) * scale_back
            out_ref[span, at : at + HD] = mixed.astype(jnp.bfloat16)


def attend(x, w, factor, bias, cosine, sines, start, kv):
    parts, rows, part = x.shape
    width = bias.shape[1]
    small = (factor, bias, cosine, sines, start, kv)
    return pl.pallas_call(
        attend_kernel,
        in_specs=[anywhere()] * 2 + [resident()] * len(small),
        out_specs=resident(),
        out_shape=jax.ShapeDtypeStruct((rows, width), jnp.bfloat16),
        scratch_shapes=[
            pltpu.VMEM(x.shape, jnp.bfloat16),
            pltpu.VMEM((parts, part, width), jnp.bfloat16),
            pltpu.SemaphoreType.DMA((2 * parts,)),
        ],
        compiler_params=params(),
        cost_estimate=pl.CostEstimate(
            flops=14_000_000_000, bytes_accessed=17_000_000, transcendentals=0
        ),
    )(x, w, *small)


def after(values, *others):
    return lax.optimization_barrier((tuple(values),) + others)[0]


def body(
    patches, window_order, vis_gain, vis_qkv, vis_qkv_bias, vis_proj, vis_proj_bias, merge_gain,
    img_owner, img_slot, prompt_rows, lang_gain, w_query, b_query, w_key, b_key, w_value, b_value,
    page_owner, page_slot,
):
    phase, rep, tp = lax.axis_index("phase"), lax.axis_index("rep"), lax.axis_index("tp")
    n_phase, n_rep = lax.axis_size("phase"), lax.axis_size("rep")
    groups = n_phase * n_rep
    group = phase * n_rep + rep
    chip, core = tp // 2, tp % 2
    bf16, f32 = jnp.bfloat16, jnp.float32

    tp_ways = lax.axis_size("tp")
    chips = tp_ways // 2
    across = lambda a, by: lax.ppermute(
        a, "tp", [(i, (i + 2 * by) % tp_ways) for i in range(tp_ways)]
    )
    partner = lambda a: lax.ppermute(a, "tp", [(i, i ^ 1) for i in range(tp_ways)])
    take = lambda a, at: lax.dynamic_index_in_dim(a, at, 0, keepdims=False)

    owner, owners = img_owner[0], page_owner[0]

    depth = w_query.shape[0]
    gain = lax.dynamic_slice_in_dim(lang_gain, group * depth, depth)[:, None]
    own = scale(gain, w_query, w_key, w_value)

    weights = lax.all_gather(own, ("phase", "rep"), axis=0, tiled=True)
    x_near = [across(prompt_rows, by) for by in (1, -1)]

    patch_count, width = patches.shape
    merge = 4
    order = window_order[0].reshape(patch_count // merge, merge).T[:, :, None]
    chunks = vis_qkv.shape[1] // VHD
    bias_pad = jnp.pad(vis_qkv_bias.reshape(chunks, VHD), ((0, 0), (0, LANE - VHD))).reshape(1, -1)
    keep, send, resid = vision_partial(
        order, patches, vis_gain, vis_qkv.T, bias_pad, vis_proj, jnp.stack([core, chip])
    )
    keep, send, resid, x_own, *x_near = after((keep, send, resid, prompt_rows, *x_near))

    x_far = across(x_own, 2)
    chip_sum = (keep.astype(f32) + partner(send).astype(f32)).astype(bf16)
    dest_iota = jnp.arange(groups, dtype=jnp.int32)
    to_images = jnp.sum(
        jnp.where(owner[None, :] == dest_iota[:, None], img_slot + 1, 0), axis=1, keepdims=True
    )
    pages = owners.shape[0]
    rows = prompt_rows.shape[0]
    page_rows = rows // pages
    page_iota = jnp.arange(pages, dtype=jnp.int32)
    first_of = lambda ids: jnp.min(
        jnp.where(ids[..., :, None] == ids[..., None, :], page_iota, pages), axis=-1
    )
    first_page = first_of(owners)
    owner_group = phase * n_rep + owners
    hit = (owner_group[None, None, :] == dest_iota[:, None, None]) & (
        (page_iota - first_page)[None, None, :] == jnp.arange(7, dtype=jnp.int32)[None, :, None]
    )
    to_pages = jnp.sum(jnp.where(hit, page_slot[0] + 1, 0), axis=2)
    routes = lax.all_to_all(
        jnp.concatenate([to_images, to_pages], axis=1), ("phase", "rep"), split_axis=0,
        concat_axis=0, tiled=True,
    )
    start = jnp.repeat(first_page, page_rows) * page_rows
    position = jnp.arange(rows, dtype=jnp.int32) - start
    half_dim = HD // 2
    inv_freq = jnp.exp(-jnp.log(1000000.0) * jnp.arange(half_dim).astype(f32) / half_dim)
    angles = position.astype(f32)[:, None] * inv_freq[None, :]
    cosine, sines = jnp.cos(angles), jnp.sin(angles)
    cosine = jnp.concatenate([cosine, cosine], axis=1)
    sines = jnp.concatenate([-sines, sines], axis=1)
    chip_sum, x_far, x_own, routes, cosine, sines = after(
        (chip_sum, x_far, x_own, routes, cosine, sines)
    )

    x_side = join(x_own, *x_near, x_far)
    ways = jnp.stack(
        [((chip - by) % chips) * 2 + side for side in (core, 1 - core) for by in (0, 1, -1, 2)]
    ).astype(jnp.int32)
    x, row_factor = ordered(ways, rows, (x_side, partner(x_side)))
    chip_sum, x, row_factor = after((chip_sum, x, row_factor))

    arrived = [across(take(chip_sum, (chip + by) % chips), by) for by in (1, -1, 2)]
    half = width // 2
    cols = lambda a: lax.dynamic_slice_in_dim(a, core * half, half, a.ndim - 1)
    mixed = resid.astype(f32) + cols(vis_proj_bias)
    for part in [take(chip_sum, chip)] + arrived:
        mixed = mixed + part.astype(f32)
    squares = jnp.sum(mixed * mixed, axis=-1).reshape(2, -1)
    squares = squares + partner(squares)
    factor = lax.rsqrt(squares.reshape(-1, 1) / width + EPS)
    merged = (mixed * factor * cols(merge_gain)).astype(bf16)
    requests = owner.shape[0]
    merged = merged.reshape(requests, -1, half)
    outgoing = place(owner, merged, groups)
    image_at = routes[:, 0] - 1
    page_at = lax.dynamic_slice_in_dim(routes, phase * n_rep, n_rep, 0)[:, 1 : 1 + CAP] - 1
    page_at = page_at.reshape(-1)
    dest = (owners * CAP + page_iota - first_page).astype(jnp.int32)
    weights, outgoing, page_at, start, dest = after(
        (weights, outgoing, page_at, start[:, None], dest)
    )

    images = lax.all_to_all(outgoing, ("phase", "rep"), split_axis=0, concat_axis=0, tiled=True)
    kv, outgoing_pages = kv_rows(
        dest, x, weights, row_factor, jnp.concatenate([b_key, b_value])[None, :], cosine, sines,
        n_rep * CAP, page_rows,
    )
    arrived_pages = lax.all_to_all(
        outgoing_pages.reshape(n_rep, CAP, page_rows, -1), "rep", split_axis=0, concat_axis=0, tiled=True
    )
    (images,) = after((images,), kv)
    image_buffer = place(image_at, images, groups).reshape(-1, half)
    attn_out = attend(x, weights, row_factor, b_query[None, :], cosine, sines, start, kv)
    kv_pool = place(page_at, arrived_pages.reshape(n_rep * CAP, page_rows, -1), pages)
    return (image_buffer, attn_out, kv_pool)


def solution(mesh):
    split, cut = P(("phase", "rep"), None), P(("phase", "rep"), "tp")
    return jax.shard_map(
        body,
        mesh=mesh,
        in_specs=(
            split, split, P(), P(None, "tp"), P("tp"), P("tp", None), P(), P(), split, split,
            cut, P(), cut, P("tp"), cut, P("tp"), cut, P("tp"), split, split,
        ),
        out_specs=(cut, cut, P(("phase", "rep"), None, "tp")),
        check_vma=False,
    )
```
